256 devices in a mesh: gx: 16 (over x, y), gy: 16 (over z, core).
Axes of the slice: x: 4, y: 4, z: 8, core: 2. Of those that a mesh axis runs over, the one named last changes fastest.
Arguments:
- surface: float32 [3, 1920, 2048], P(None, 'gy', 'gx'), may hold values from -5 to 5
- depth: float32 [1920, 2048], P('gy', 'gx'), may hold values from 0.05 to 0.4
- coriolis: float32 [1920, 2048], P('gy', 'gx'), may hold values from -0.3 to 0.3
- land_sea: int32 [1920, 2048], P('gy', 'gx'), may hold values 0 or 1
- basis: bfloat16 [64, 3, 1920, 2048], P(None, None, 'gy', 'gx'), may hold values from -8 to 8
- energies: float32 [64], replicated, may hold values from 0.5 to 2
- start: float32 [68, 64], replicated, may hold values from -6 to 6
Outputs:
- final_state: float32 [3, 1920, 2048], P(None, 'gy', 'gx')
- projected: bfloat16 [64, 3, 1920, 2048], P(None, None, 'gy', 'gx')
The draws below stay inside these ranges and needn't reach their ends.
All inputs are finite; a program needn't handle non-finite values. No bound on the sum of `land_sea` on one device may be relied on, other than what follows from the above.
Results may differ from the reference program's by a relative error of at most 0.0049.
Values sent between devices are 32-bit elements; how exact they have to be, the bound alone decides.
No kernel may reach another device: no remote copies, remote signals or barrier semaphores. Data moves between devices by JAX's collectives and lax.ppermute only.
A program may use at most 128 MiB of HBM per device.

```python
import math
import jax
import jax.numpy as jnp
from jax import lax

CY = 120
RANK = 64
SNAPS = 4
STEPS = 8
SUBITER = 6
KCOLS = 68
NY = 1920
NX = 2048


def normal_field(key, scale):
    return scale * jax.random.truncated_normal(key, -7.0, 7.0, (3, NY, NX), jnp.float32)


def draw_surface(key, part):
    field = normal_field(key, 0.7)
    return field


def draw_basis(key, part):
    common = normal_field(key, 0.7)
    key = jax.random.fold_in(key, 5)
    mix_key, lift_key, noise_key = jax.random.split(key, 3)
    mixing = jax.random.truncated_normal(mix_key, -3.0, 3.0, (RANK, RANK), jnp.float32)
    lifts = 0.35 * jax.random.truncated_normal(lift_key, -3.0, 3.0, (RANK,), jnp.float32)
    blocks = NY // CY

    def one_block(index):
        block_key = jax.random.fold_in(noise_key, index)
        noise = jax.random.truncated_normal(block_key, -4.0, 4.0, (RANK, 3, CY, NX), jnp.float32)
        mixed = jnp.einsum('rm,mfyx->rfyx', mixing, noise, precision=lax.Precision.HIGHEST)
        piece = lax.dynamic_slice_in_dim(common, (index * CY).astype(jnp.int32), CY, 1)
        total = noise + 0.025 * mixed + lifts[:, None, None, None] * piece[None]
        return jnp.clip(total, -8.0, 8.0).astype(jnp.bfloat16)
    pieces = lax.map(one_block, jnp.arange(blocks, dtype=jnp.int32))
    return jnp.moveaxis(pieces, 0, 2).reshape(RANK, 3, NY, NX)


def with_ends(values, key, smallest, high):
    place = [jax.random.randint(jax.random.fold_in(key, axis), (), 0, length) for axis, length in enumerate(values.shape)]
    longest = values.shape.index(max(values.shape))
    beside = place[:longest] + [(place[longest] + 1) % values.shape[longest]] + place[longest + 1:]
    return values.at[tuple(place)].set(smallest).at[tuple(beside)].set(high)


def steps_of(own_key, dims, cuts, low, high):
    def one(position, shards_of):
        draws = jax.random.uniform(jax.random.fold_in(jax.random.fold_in(own_key, 6), position), (shards_of,), jnp.float32, low / len(cuts), high / len(cuts))
        return jnp.repeat(jnp.exp(draws), dims[position] // shards_of).reshape((-1,) + (1,) * (len(dims) - position - 1))

    gain = one(*cuts[0])
    for cut in cuts[1:]:
        gain = gain * one(*cut)
    return gain


def centred(key, dims, width, limit, held_as=jnp.bfloat16):
    entries = jax.random.normal(key, dims, jnp.float32) * width
    return jnp.minimum(jnp.maximum(entries, -limit), limit).astype(held_as)


def setup_inputs(seed: int = 0) -> dict:
    streams_of = jax.random.split(jax.random.key(seed), 8)
    surface = draw_surface(jax.random.fold_in(streams_of[7], 71), 0)
    depth = jnp.clip(jnp.exp(math.log(0.4) - 2.0794415 * jax.random.uniform(streams_of[1], (NY, NX), jnp.float32) ** steps_of(streams_of[1], (NY, NX), ((0, 16), (1, 16)), -0.2, 0.2)), 0.05, 0.4)
    coriolis = jnp.clip(jax.random.uniform(streams_of[2], (NY, NX), jnp.float32, -0.3, 0.3) * steps_of(streams_of[2], (NY, NX), ((0, 16), (1, 16)), -0.4, 0.0), -0.3, 0.3)
    land_sea = with_ends((jax.random.randint(streams_of[3], (NY, NX), 0, 10) < 9).astype(jnp.int32), jax.random.fold_in(streams_of[3], 1), 0, 1)
    basis = draw_basis(jax.random.fold_in(streams_of[7], 71), 0)
    energies = jnp.clip(jnp.exp(jax.random.uniform(streams_of[5], (RANK,), jnp.float32, math.log(0.5), math.log(2.0))), 0.5, 2.0)
    start = centred(streams_of[6], (KCOLS, RANK), 1.0, 6.0, jnp.float32)
    return dict(surface=surface, depth=depth, coriolis=coriolis, land_sea=land_sea, basis=basis, energies=energies, start=start)


def east(field):
    return jnp.roll(field, -1, axis=1)

def west(field):
    return jnp.roll(field, 1, axis=1)

def north(field):
    return jnp.concatenate([field[1:], jnp.zeros_like(field[:1])], axis=0)

def south(field):
    return jnp.concatenate([jnp.zeros_like(field[:1]), field[:-1]], axis=0)

def refine(gram, start):
    coeffs = start
    for sweep in range(SUBITER):
        images = jnp.dot(gram, coeffs, precision=lax.Precision.HIGHEST)
        inner = jnp.dot(images.T, images, precision=lax.Precision.HIGHEST)
        lower = jnp.linalg.cholesky(inner)
        coeffs = lax.linalg.triangular_solve(lower, images, left_side=False, lower=True, transpose_a=True)
    return coeffs

def reference(surface, depth, coriolis, land_sea, basis, energies, start):
    wet_cells = land_sea.astype(jnp.float32)
    zonal_open = wet_cells * east(wet_cells)
    north_open = wet_cells * north(wet_cells)
    zonal_depth = 0.5 * (depth + east(depth))
    north_depth = 0.5 * (depth + north(depth))
    height, zonal, merid = (surface[0], surface[1], surface[2])
    frames = []
    for turn_index in range(STEPS):
        zonal_flux = zonal_depth * zonal
        north_flux = north_depth * merid
        height = height - (zonal_flux - west(zonal_flux)) - (north_flux - south(north_flux))
        vbar = 0.25 * (merid + east(merid) + south(merid) + south(east(merid)))
        zonal = zonal_open * (zonal - (east(height) - height) + coriolis * vbar)
        ubar = 0.25 * (zonal + west(zonal) + north(zonal) + north(west(zonal)))
        merid = north_open * (merid - (north(height) - height) - coriolis * ubar)
        if (turn_index + 1) % (STEPS // SNAPS) == 0:
            frames.append(jnp.stack([height, zonal, merid]).astype(jnp.bfloat16))
    final_state = jnp.stack([height, zonal, merid])
    snapshots = jnp.stack(frames)
    blocks = NY // CY

    def block_matrix(index):
        first = (index * CY).astype(jnp.int32)
        base_part = lax.dynamic_slice_in_dim(basis, first, CY, 2).reshape(RANK, -1)
        snap_part = lax.dynamic_slice_in_dim(snapshots, first, CY, 2).reshape(SNAPS, -1)
        return jnp.concatenate([base_part, snap_part], axis=0)

    def add_block(total, index):
        matrix = block_matrix(index)
        term = lax.dot_general(matrix.astype(jnp.float32), matrix.astype(jnp.float32), (((1,), (1,)), ((), ())), preferred_element_type=jnp.float32)
        return (total + term, None)
    gram0, unused = lax.scan(add_block, jnp.zeros((KCOLS, KCOLS), jnp.float32), jnp.arange(blocks, dtype=jnp.int32))
    weights = jnp.concatenate([energies, jnp.ones((SNAPS,), jnp.float32)])
    gram = gram0 * (weights[:, None] * weights[None, :]) / (3.0 * NY * NX)
    coeffs = refine(gram, start)
    scaled = (weights[:, None] * coeffs).astype(jnp.bfloat16)

    def project_block(index):
        matrix = block_matrix(index)
        result = jnp.dot(scaled.T.astype(jnp.float32), matrix.astype(jnp.float32), preferred_element_type=jnp.float32)
        return result.astype(jnp.bfloat16).reshape(RANK, 3, CY, NX)
    pieces = lax.map(project_block, jnp.arange(blocks, dtype=jnp.int32))
    projected = jnp.moveaxis(pieces, 0, 2).reshape(RANK, 3, NY, NX)
    return (final_state, projected)
```

```python
import jax
import jax.numpy as jnp
from jax import lax
from jax.experimental import pallas as pl
from jax.experimental.pallas import tpu as pltpu
from jax.sharding import PartitionSpec as P

RANK = 64
SNAPS = 4
STEPS = 8
SUBITER = 6
KCOLS = RANK + SNAPS
FIELDS = 6
WIDE = 9
PITCH = 21
HALO = 8
VMEM_LIMIT = 48 * 1024 * 1024


def pack_lane(shape, field):
    lane = lax.broadcasted_iota(jnp.int32, shape, 1)
    return (lane + (WIDE - PITCH * field) % 128) & 127


def field_values(surface, depth, coriolis, land_sea):
    return (
        surface[0],
        surface[1],
        surface[2],
        coriolis[...],
        land_sea[...].astype(jnp.float32),
        depth[...],
    )


def pack_kernel(surface, depth, coriolis, land_sea, packed):
    total = jnp.zeros(packed.shape, jnp.float32)
    for field, value in enumerate(field_values(surface, depth, coriolis, land_sea)):
        if field:
            value = pltpu.roll(value, PITCH * field, 1)
        total = jnp.where(pack_lane(packed.shape, field) < 2 * WIDE, value, total)
    packed[...] = total


def combined(from_west, from_east):
    west = pack_lane(from_west.shape, 0) < WIDE
    for field in range(1, FIELDS):
        west = west | (pack_lane(from_west.shape, field) < WIDE)
    return jnp.where(west, from_west, from_east)


def rows_kernel(
    surface_low, depth_low, coriolis_low, land_low, west_low, east_low,
    surface_high, depth_high, coriolis_high, land_high, west_high, east_high,
    to_south, to_north,
):
    ones = jnp.ones((HALO, 128), jnp.float32)
    low = field_values(surface_low, depth_low, coriolis_low, land_low)
    halo_low = combined(west_low[...], east_low[...])
    blocks = [value[:HALO] for value in low]
    blocks += [halo_low[:HALO], low[-1][HALO:], halo_low[HALO:], ones]
    for index, block in enumerate(blocks):
        to_south[index * HALO : (index + 1) * HALO, :] = block
    high = field_values(surface_high, depth_high, coriolis_high, land_high)
    blocks = list(high) + [combined(west_high[...], east_high[...])]
    for index, block in enumerate(blocks):
        to_north[index * HALO : (index + 1) * HALO, :] = block


def window_kernel(
    surface, depth, coriolis, land_sea, from_west, from_east, from_north, from_south,
    state, snaps, height, zonal, merid, statics,
):
    rows = depth.shape[0]
    tall = rows + 2 * HALO
    halo = jnp.concatenate(
        [
            from_south[FIELDS * HALO :, :],
            combined(from_west[...], from_east[...]),
            from_north[FIELDS * HALO : (FIELDS + 1) * HALO, :],
        ],
        axis=0,
    )

    def extended(field, value):
        span = slice(field * HALO, (field + 1) * HALO)
        main = jnp.concatenate([from_south[span, :], value, from_north[span, :]], axis=0)
        side = pltpu.roll(halo, 128 - PITCH * field, 1) if field else halo
        return jnp.concatenate([main, side], axis=1)

    def east(value):
        return pltpu.roll(value, 255, 1)

    def west(value):
        return pltpu.roll(value, 1, 1)

    def north(value):
        return pltpu.roll(value, tall - 1, 0)

    def south(value):
        return pltpu.roll(value, 1, 0)

    values = field_values(surface, depth, coriolis, land_sea)
    for ref, field in ((height, 0), (zonal, 1), (merid, 2)):
        ref[...] = extended(field, values[field])
    statics[0] = extended(3, values[3])
    wet = extended(4, values[4])
    statics[1] = wet * east(wet)
    statics[2] = wet * north(wet)
    deep = extended(5, values[5])
    statics[3] = 0.5 * (deep + east(deep))
    side = pltpu.roll(from_north[(FIELDS + 2) * HALO : (FIELDS + 3) * HALO, :], 128 - PITCH * 5, 1)
    above = jnp.concatenate([from_north[(FIELDS + 1) * HALO : (FIELDS + 2) * HALO, :], side], axis=1)
    row = lax.broadcasted_iota(jnp.int32, (tall, 256), 0)
    upper = jnp.where(row == tall - 1, above[:1], north(deep))
    statics[4] = 0.5 * (deep + upper)
    there = from_north[(FIELDS + 3) * HALO :, :]
    there = jnp.concatenate([there, there], axis=1)

    def one_step():
        flux = statics[3] * zonal[...]
        drop = statics[4] * merid[...]
        high = height[...] - (flux - west(flux)) - (drop - south(drop))
        high = jnp.concatenate([high[: tall - HALO], high[tall - HALO :] * there], axis=0)
        height[...] = high
        across = merid[...]
        across = across + east(across)
        vbar = 0.25 * (across + south(across))
        flow = statics[1] * (zonal[...] - (east(high) - high) + statics[0] * vbar)
        zonal[...] = flow
        across = flow + west(flow)
        ubar = 0.25 * (across + north(across))
        merid[...] = statics[2] * (merid[...] - (north(high) - high) - statics[0] * ubar)

    def some_steps(turn, carry):
        for _ in range(STEPS // SNAPS):
            one_step()
        for index, ref in enumerate((height, zonal, merid)):
            snaps[turn, index] = ref[HALO : HALO + rows, :128].astype(jnp.bfloat16)
        return carry

    lax.fori_loop(0, SNAPS, some_steps, 0)
    for index, ref in enumerate((height, zonal, merid)):
        state[index] = ref[HALO : HALO + rows, :128]


def window(surface, depth, coriolis, land_sea):
    rows, cols = depth.shape
    whole = pltpu.CompilerParams(vmem_limit_bytes=VMEM_LIMIT)
    packed = pl.pallas_call(
        pack_kernel,
        out_shape=jax.ShapeDtypeStruct((rows, cols), jnp.float32),
        compiler_params=whole,
    )(surface, depth, coriolis, land_sea)
    around = lax.axis_size("gx")
    from_west = lax.ppermute(packed, "gx", [(i, (i + 1) % around) for i in range(around)])
    from_east = lax.ppermute(packed, "gx", [(i, (i - 1) % around) for i in range(around)])
    fields = (surface, depth, coriolis, land_sea, from_west, from_east)

    def strips(height, index):
        return [
            pl.BlockSpec((3, height, cols), lambda i: (0, index, 0))
            if value.ndim == 3
            else pl.BlockSpec((height, cols), lambda i: (index, 0))
            for value in fields
        ]

    to_south, to_north = pl.pallas_call(
        rows_kernel,
        grid=(1,),
        in_specs=strips(2 * HALO, 0) + strips(HALO, rows // HALO - 1),
        out_shape=(
            jax.ShapeDtypeStruct(((FIELDS + 4) * HALO, cols), jnp.float32),
            jax.ShapeDtypeStruct(((FIELDS + 1) * HALO, cols), jnp.float32),
        ),
        compiler_params=whole,
    )(*fields, *fields)
    up = lax.axis_size("gy")
    from_north = lax.ppermute(to_south, "gy", [(i, i - 1) for i in range(1, up)])
    from_south = lax.ppermute(to_north, "gy", [(i, i + 1) for i in range(up - 1)])
    tall = (rows + 2 * HALO, 2 * cols)
    return pl.pallas_call(
        window_kernel,
        out_shape=(
            jax.ShapeDtypeStruct((3, rows, cols), jnp.float32),
            jax.ShapeDtypeStruct((SNAPS, 3, rows, cols), jnp.bfloat16),
        ),
        scratch_shapes=[pltpu.VMEM(tall, jnp.float32)] * 3 + [pltpu.VMEM((5,) + tall, jnp.float32)],
        compiler_params=whole,
    )(*fields, from_north, from_south)


def over_cells(left, right):
    return lax.dot_general(
        left, right, (((1, 2, 3), (1, 2, 3)), ((), ())), preferred_element_type=jnp.float32
    )


def pair_sum(value, axis, partner):
    return value + lax.ppermute(value, axis, [(i, partner(i)) for i in range(16)])


def total_over_devices(value):
    rings = (
        lambda a: a ^ 1,
        lambda a: ((a - 1) ^ 1) + 1 if 0 < a < 7 else 7 - a,
        lambda a: (7 - a) if a in (1, 2, 5, 6) else {0: 3, 3: 0, 4: 7, 7: 4}[a],
    )
    value = pair_sum(value, "gy", lambda i: i ^ 1)
    for ring in rings:
        value = pair_sum(value, "gy", lambda i, ring=ring: ring(i // 2) * 2 + i % 2)
    spread = jnp.broadcast_to(value[None], (16,) + value.shape)
    return lax.all_to_all(spread, "gx", 0, 0, tiled=True).sum(0)


def exact_dot(left, right, dims=(((1,), (0,)), ((), ()))):
    return lax.dot_general(
        left, right, dims, precision=lax.Precision.HIGHEST, preferred_element_type=jnp.float32
    )


def refine(gram, start, weights, result):
    blocks = RANK // 8
    sweep = lax.broadcasted_iota(jnp.int32, (8, 128), 0)
    made = None
    past = []
    for time in range(blocks + SUBITER - 1):
        inputs = []
        for i in range(8):
            value = jnp.zeros((8, 128), jnp.float32) if made is None else pltpu.roll(made[i], 1, 0)
            if time < blocks:
                value = jnp.where(sweep == 0, start[8 * time + i : 8 * time + i + 1, :], value)
            inputs.append(value)
        active = (sweep <= time) & (sweep > time - blocks) & (sweep < SUBITER)
        images = exact_dot(jnp.concatenate(inputs, axis=0), gram)
        if past:
            history = jnp.concatenate(past[-(blocks - 1) :], axis=0)
            inner = exact_dot(images, history, (((1,), (1,)), ((), ())))
            row = lax.broadcasted_iota(jnp.int32, inner.shape, 0)
            col = lax.broadcasted_iota(jnp.int32, inner.shape, 1)
            inner = jnp.where((row & 7) == (col & 7), inner, 0.0)
            images = images - exact_dot(inner, history)
        parts = [images[8 * i : 8 * i + 8] for i in range(8)]
        square = {
            (i, j): jnp.sum(parts[i] * parts[j], axis=1, keepdims=True)
            for i in range(8)
            for j in range(i, 8)
        }
        made = []
        for i in range(8):
            scale = lax.rsqrt(square[i, i])
            unit = parts[i] * scale
            made.append(jnp.where(active, unit, 0.0))
            lower = {j: square[i, j] * scale for j in range(i + 1, 8)}
            for j in range(i + 1, 8):
                parts[j] = parts[j] - lower[j] * unit
                for p in range(j, 8):
                    square[j, p] = square[j, p] - lower[j] * lower[p]
        past.append(jnp.concatenate(made, axis=0))
        first = time - (SUBITER - 1)
        if first >= 0:
            for i in range(8):
                result[8 * first + i : 8 * first + i + 1, :] = made[i][SUBITER - 1 : SUBITER] * weights


def finish_kernel(
    sums, outer, start, weights, snaps, basis, projected, base, out, coeffs, spread, spread_snaps, load_sems, store_sems
):
    rows = base.shape[2]
    loads = [pltpu.make_async_copy(basis.at[:, f], base.at[:, f], load_sems.at[f]) for f in range(3)]
    stores = [pltpu.make_async_copy(out.at[:, f], projected.at[:, f], store_sems.at[f]) for f in range(3)]
    for load in loads:
        load.start()
    half = RANK // 2
    low = sums[:half]
    lane = lax.broadcasted_iota(jnp.int32, (half, 128), 1)
    upper = jnp.where(lane < RANK, low, 0.0)
    under = jnp.where(lane < RANK, pltpu.roll(low, 128 - RANK, 1), 0.0)
    cross = sums[half : half + 8]
    rest = jnp.zeros((RANK - 8, 128), jnp.float32)
    lane = lax.broadcasted_iota(jnp.int32, (8, 128), 1)
    corner = jnp.where(lane < RANK, 0.0, cross)
    border = jnp.where(lane < RANK, cross, 0.0)
    flat = jnp.zeros((RANK, 128), jnp.float32)
    mirrored = jnp.transpose(jnp.concatenate([flat, border, rest], axis=0), (1, 0))
    gram = jnp.concatenate([upper, under, corner + border, rest], axis=0) + mirrored
    refine(gram * outer[...], start, weights[...], coeffs)

    scaled = coeffs[...].astype(jnp.bfloat16)
    tall = RANK * 8
    repeated = jnp.broadcast_to(coeffs[...][:, None, :], (RANK, 8, 128)).reshape(tall, 128).astype(jnp.bfloat16)
    del scaled

    def widened(first, count):
        k = lax.broadcasted_iota(jnp.int32, (128, count * 8), 0)
        col = lax.broadcasted_iota(jnp.int32, (128, count * 8), 1)
        pick = jnp.where(k - first == lax.shift_right_logical(col, 3), 1.0, 0.0).astype(jnp.bfloat16)
        wide = jnp.dot(repeated, pick, preferred_element_type=jnp.float32)
        row = lax.broadcasted_iota(jnp.int32, wide.shape, 0)
        col = lax.broadcasted_iota(jnp.int32, wide.shape, 1)
        return jnp.where((row & 7) == (col & 7), wide, 0.0).astype(jnp.bfloat16)

    spread[...] = widened(0, RANK)
    spread_snaps[...] = widened(RANK, SNAPS)

    def mixed(field, first, count):
        def tile(ref, kinds):
            value = ref[:, field, pl.ds(first, count), :].astype(jnp.float32)
            halves = [value[:, 8 * h : 8 * h + 8].reshape(kinds * 8, 128) for h in range(count // 8)]
            return (halves[0] if count == 8 else jnp.concatenate(halves, axis=1)).astype(jnp.bfloat16)

        total = jnp.dot(spread[...], tile(base, RANK), preferred_element_type=jnp.float32)
        total = total + jnp.dot(spread_snaps[...], tile(snaps, SNAPS), preferred_element_type=jnp.float32)
        halves = [total[:, 128 * h : 128 * h + 128].reshape(RANK, 8, 128) for h in range(count // 8)]
        total = halves[0] if count == 8 else jnp.concatenate(halves, axis=1)
        out[:, field, pl.ds(first, count), :] = total.astype(jnp.bfloat16)

    for field in range(3):
        loads[field].wait()

        def pair(index, carry, field=field):
            mixed(field, pl.multiple_of(index * 16, 16), 16)
            return carry

        lax.fori_loop(0, rows // 16, pair, 0)
        if rows % 16:
            mixed(field, rows - 8, 8)
        stores[field].start()
    for store in stores:
        store.wait()


def local(surface, depth, coriolis, land_sea, basis, energies, start):
    rows, cols = depth.shape
    final_state, snaps = window(surface, depth, coriolis, land_sea)
    gram_base = over_cells(basis, basis)
    cross = over_cells(snaps, basis)
    square = over_cells(snaps, snaps)
    half = RANK // 2
    sums = jnp.concatenate(
        [
            jnp.concatenate([gram_base[:half], gram_base[half:]], axis=1),
            jnp.pad(jnp.concatenate([cross, square], axis=1), ((0, 4), (0, 128 - KCOLS))),
        ],
        axis=0,
    )
    sums = total_over_devices(sums)
    cells = 3.0 * rows * cols * lax.axis_size("gx") * lax.axis_size("gy")
    weights = jnp.concatenate([energies, jnp.ones((SNAPS,), jnp.float32)])
    weights = jnp.pad(weights, (0, 128 - KCOLS))
    outer = weights[:, None] * weights[None, :] / cells
    turned = jnp.pad(start.T, ((0, 0), (0, 128 - KCOLS)))
    vmem = pl.BlockSpec(memory_space=pltpu.VMEM)
    projected = pl.pallas_call(
        finish_kernel,
        in_specs=[vmem] * 5 + [pl.BlockSpec(memory_space=pl.ANY)],
        out_specs=pl.BlockSpec(memory_space=pl.ANY),
        out_shape=jax.ShapeDtypeStruct(basis.shape, jnp.bfloat16),
        scratch_shapes=[
            pltpu.VMEM(basis.shape, jnp.bfloat16),
            pltpu.VMEM(basis.shape, jnp.bfloat16),
            pltpu.VMEM((RANK, 128), jnp.float32),
            pltpu.VMEM((RANK * 8, RANK * 8), jnp.bfloat16),
            pltpu.VMEM((RANK * 8, SNAPS * 8), jnp.bfloat16),
            pltpu.SemaphoreType.DMA((3,)),
            pltpu.SemaphoreType.DMA((3,)),
        ],
        compiler_params=pltpu.CompilerParams(vmem_limit_bytes=VMEM_LIMIT),
    )(sums, outer, turned, weights[None, :], snaps, basis)
    return (final_state, projected)


def solution(mesh):
    placed = (
        P(None, "gy", "gx"),
        P("gy", "gx"),
        P("gy", "gx"),
        P("gy", "gx"),
        P(None, None, "gy", "gx"),
        P(),
        P(),
    )
    return jax.shard_map(
        local,
        mesh=mesh,
        in_specs=placed,
        out_specs=(P(None, "gy", "gx"), P(None, None, "gy", "gx")),
        check_vma=False,
    )
```

```python
import jax
import jax.numpy as jnp
from jax import lax
from jax.experimental import pallas as pl
from jax.experimental.pallas import tpu as pltpu
from jax.sharding import PartitionSpec as P

RANK = 64
SNAPS = 4
STEPS = 8
SUBITER = 6
KCOLS = RANK + SNAPS
FIELDS = 6
WIDE = 9
PITCH = 21
HALO = 8
VMEM_LIMIT = 40 * 1024 * 1024


def pack_lane(shape, field):
    lane = lax.broadcasted_iota(jnp.int32, shape, 1)
    return (lane + (WIDE - PITCH * field) % 128) & 127


def pack_kernel(fields, packed):
    total = jnp.zeros(packed.shape, jnp.float32)
    for field in range(FIELDS):
        value = fields[field]
        if field:
            value = pltpu.roll(value, PITCH * field, 1)
        total = jnp.where(pack_lane(packed.shape, field) < 2 * WIDE, value, total)
    packed[...] = total


def combined(first, second, odd):
    west = pack_lane(first.shape, 0) < WIDE
    for field in range(1, FIELDS):
        west = west | (pack_lane(first.shape, field) < WIDE)
    return jnp.where(west == (odd == 0), second, first)


def odd_of(axis):
    return lax.axis_index(axis) & 1


def rows_kernel(fields_low, first_low, second_low, fields_high, first_high, second_high, send_first, send_second):
    odd = odd_of("gx")
    halo_low = combined(first_low[...], second_low[...], odd)
    to_south = [fields_low[field, :HALO] for field in range(FIELDS)]
    to_south += [halo_low[:HALO], fields_low[FIELDS - 1, HALO:], halo_low[HALO:]]
    to_south += [jnp.ones((HALO, 128), jnp.float32)]
    to_north = [fields_high[field] for field in range(FIELDS)]
    to_north += [combined(first_high[...], second_high[...], odd)]
    to_north += [jnp.zeros((HALO, 128), jnp.float32)] * (len(to_south) - len(to_north))
    upper = odd_of("gy") == 1
    for index, (south, north) in enumerate(zip(to_south, to_north)):
        span = slice(index * HALO, (index + 1) * HALO)
        send_first[span, :] = jnp.where(upper, south, north)
        send_second[span, :] = jnp.where(upper, north, south)


def window_kernel(
    fields, first_side, second_side, first_rows, second_rows,
    state, snaps, height, zonal, merid, statics, frames,
):
    rows = fields.shape[1]
    tall = rows + 2 * HALO
    upper = odd_of("gy") == 1
    from_north = jnp.where(upper, second_rows[...], first_rows[...])
    from_south = jnp.where(upper, first_rows[...], second_rows[...])
    halo = jnp.concatenate(
        [
            from_south[FIELDS * HALO : (FIELDS + 1) * HALO, :],
            combined(first_side[...], second_side[...], odd_of("gx")),
            from_north[FIELDS * HALO : (FIELDS + 1) * HALO, :],
        ],
        axis=0,
    )

    def extended(field, value):
        span = slice(field * HALO, (field + 1) * HALO)
        main = jnp.concatenate([from_south[span, :], value, from_north[span, :]], axis=0)
        side = pltpu.roll(halo, 128 - PITCH * field, 1) if field else halo
        return jnp.concatenate([main, side], axis=1)

    def east(value):
        return pltpu.roll(value, 255, 1)

    def west(value):
        return pltpu.roll(value, 1, 1)

    def north(value):
        return pltpu.roll(value, tall - 1, 0)

    def south(value):
        return pltpu.roll(value, 1, 0)

    values = [fields[field] for field in range(FIELDS)]
    for ref, field in ((height, 0), (zonal, 1), (merid, 2)):
        ref[...] = extended(field, values[field])
    statics[0] = extended(3, values[3])
    wet = extended(4, values[4])
    statics[1] = wet * east(wet)
    statics[2] = wet * north(wet)
    deep = extended(5, values[5])
    statics[3] = 0.5 * (deep + east(deep))
    side = pltpu.roll(from_north[(FIELDS + 2) * HALO : (FIELDS + 3) * HALO, :], 128 - PITCH * 5, 1)
    above = jnp.concatenate([from_north[(FIELDS + 1) * HALO : (FIELDS + 2) * HALO, :], side], axis=1)
    row = lax.broadcasted_iota(jnp.int32, (tall, 256), 0)
    upper = jnp.where(row == tall - 1, above[:1], north(deep))
    statics[4] = 0.5 * (deep + upper)
    there = from_north[(FIELDS + 3) * HALO :, :]
    there = jnp.concatenate([there, there], axis=1)

    def one_step():
        flux = statics[3] * zonal[...]
        drop = statics[4] * merid[...]
        high = height[...] - (flux - west(flux)) - (drop - south(drop))
        high = jnp.concatenate([high[: tall - HALO], high[tall - HALO :] * there], axis=0)
        height[...] = high
        across = merid[...]
        across = across + east(across)
        vbar = 0.25 * (across + south(across))
        flow = statics[1] * (zonal[...] - (east(high) - high) + statics[0] * vbar)
        zonal[...] = flow
        across = flow + west(flow)
        ubar = 0.25 * (across + north(across))
        merid[...] = statics[2] * (merid[...] - (north(high) - high) - statics[0] * ubar)

    def some_steps(turn, carry):
        for _ in range(STEPS // SNAPS):
            one_step()
        for index, ref in enumerate((height, zonal, merid)):
            place = pl.ds(index * rows * 8 + turn, rows, stride=8)
            frames[place, :] = ref[HALO : HALO + rows, :128]
        return carry

    frames[...] = jnp.zeros(frames.shape, jnp.float32)

    lax.fori_loop(0, SNAPS, some_steps, 0)
    for index, ref in enumerate((height, zonal, merid)):
        state[index] = ref[HALO : HALO + rows, :128]
    snaps[...] = frames[...].reshape(snaps.shape).astype(jnp.bfloat16)


def pairs(offset, around):
    partners = [(i, (((i - offset) ^ 1) + offset) % 16) for i in range(16)]
    return [(i, j) for i, j in partners if around or abs(i - j) == 1]


def window(surface, depth, coriolis, land_sea, basis):
    rows, cols = depth.shape
    whole = pltpu.CompilerParams(vmem_limit_bytes=VMEM_LIMIT)
    wet = land_sea.astype(jnp.float32)
    fields = jnp.concatenate([surface, coriolis[None], wet[None], depth[None]], axis=0)
    packed = pl.pallas_call(
        pack_kernel,
        out_shape=jax.ShapeDtypeStruct((rows, cols), jnp.float32),
        compiler_params=whole,
    )(fields)
    sides = [lax.ppermute(packed, "gx", pairs(offset, True)) for offset in (0, 1)]

    turned = jnp.transpose(basis, (1, 2, 0, 3)).reshape(3 * rows, RANK, cols)
    turned, sides = lax.optimization_barrier((turned, sides))

    def strips(height, index):
        side = pl.BlockSpec((height, cols), lambda i: (index, 0))
        return [pl.BlockSpec((FIELDS, height, cols), lambda i: (0, index, 0)), side, side]

    slab = jax.ShapeDtypeStruct(((FIELDS + 4) * HALO, cols), jnp.float32)
    sends = pl.pallas_call(
        rows_kernel,
        grid=(1,),
        in_specs=strips(2 * HALO, 0) + strips(HALO, rows // HALO - 1),
        out_shape=(slab, slab),
        compiler_params=whole,
    )(fields, *sides, fields, *sides)
    turned, sends = lax.optimization_barrier((turned, sends))
    gram_base = over_cells(turned, turned)
    slabs = [lax.ppermute(send, "gy", pairs(offset, False)) for offset, send in enumerate(sends)]
    tall = (rows + 2 * HALO, 2 * cols)
    final_state, snaps = pl.pallas_call(
        window_kernel,
        out_shape=(
            jax.ShapeDtypeStruct((3, rows, cols), jnp.float32),
            jax.ShapeDtypeStruct((3 * rows, 8, cols), jnp.bfloat16),
        ),
        scratch_shapes=[pltpu.VMEM(tall, jnp.float32)] * 3
        + [pltpu.VMEM((5,) + tall, jnp.float32), pltpu.VMEM((3 * rows * 8, cols), jnp.float32)],
        compiler_params=whole,
    )(fields, *sides, *slabs)
    return final_state, snaps, turned, gram_base


def over_cells(left, right):
    return lax.dot_general(
        left, right, (((0, 2), (0, 2)), ((), ())), preferred_element_type=jnp.float32
    )


def exchanged(value, axis, partner):
    return lax.ppermute(value, axis, [(i, partner(i)) for i in range(16)])


def quad_sum(value, axis, one, two):
    first = exchanged(value, axis, lambda i: i ^ one)
    second = exchanged(value, axis, lambda i: i ^ two)
    third = exchanged(value, axis, lambda i: i ^ one ^ two)
    return (value + first) + (second + third)


def total_over_devices(value):
    value = quad_sum(value, "gy", 1, 2)
    ring = lambda a: ((a - 1) ^ 1) + 1 if 0 < a < 7 else 7 - a
    value = value + exchanged(value, "gy", lambda i: ring(i // 2) * 2 + i % 2)
    ring = lambda a: (7 - a) if a in (1, 2, 5, 6) else {0: 3, 3: 0, 4: 7, 7: 4}[a]
    value = value + exchanged(value, "gy", lambda i: ring(i // 2) * 2 + i % 2)
    value = quad_sum(value, "gx", 1, 4)
    return quad_sum(value, "gx", 3, 12)


def exact_dot(left, right, dims=(((1,), (0,)), ((), ()))):
    return lax.dot_general(
        left, right, dims, precision=lax.Precision.HIGHEST, preferred_element_type=jnp.float32
    )


def refine(gram, start, weights, result):
    blocks = RANK // 8
    sweep = lax.broadcasted_iota(jnp.int32, (8, 128), 0)
    made = None
    past = []
    for time in range(blocks + SUBITER - 1):
        inputs = []
        for i in range(8):
            value = jnp.zeros((8, 128), jnp.float32) if made is None else pltpu.roll(made[i], 1, 0)
            if time < blocks:
                value = jnp.where(sweep == 0, start[8 * time + i : 8 * time + i + 1, :], value)
            inputs.append(value)
        active = (sweep <= time) & (sweep > time - blocks) & (sweep < SUBITER)
        images = exact_dot(jnp.concatenate(inputs, axis=0), gram)
        if past:
            history = jnp.concatenate(past[-(blocks - 1) :], axis=0)
            inner = exact_dot(images, history, (((1,), (1,)), ((), ())))
            row = lax.broadcasted_iota(jnp.int32, inner.shape, 0)
            col = lax.broadcasted_iota(jnp.int32, inner.shape, 1)
            inner = jnp.where((row & 7) == (col & 7), inner, 0.0)
            images = images - exact_dot(inner, history)
        parts = [images[8 * i : 8 * i + 8] for i in range(8)]
        square = {
            (i, j): jnp.sum(parts[i] * parts[j], axis=1, keepdims=True)
            for i in range(8)
            for j in range(i, 8)
        }
        made = []
        for i in range(8):
            scale = lax.rsqrt(square[i, i])
            unit = parts[i] * scale
            made.append(jnp.where(active, unit, 0.0))
            lower = {j: square[i, j] * scale for j in range(i + 1, 8)}
            for j in range(i + 1, 8):
                parts[j] = parts[j] - lower[j] * unit
                for p in range(j, 8):
                    square[j, p] = square[j, p] - lower[j] * lower[p]
        past.append(jnp.concatenate(made, axis=0))
        first = time - (SUBITER - 1)
        if first >= 0:
            for i in range(8):
                result[8 * first + i : 8 * first + i + 1, :] = made[i][SUBITER - 1 : SUBITER] * weights


def crossed(eight):
    eight = list(eight)
    row = lax.broadcasted_iota(jnp.int32, eight[0].shape, 1)
    for step in (4, 2, 1):
        keep = (row & step) == 0
        for i in range(8):
            if i & step == 0:
                low, high = eight[i], eight[i + step]
                eight[i] = jnp.where(keep, low, pltpu.roll(high, step, 1))
                eight[i + step] = jnp.where(keep, pltpu.roll(low, 8 - step, 1), high)
    return eight


def finish_kernel(sums, outer, start, weights, snaps, turned, projected, out, coeffs, store_sems):
    rows = out.shape[2]
    stores = [pltpu.make_async_copy(out.at[:, f], projected.at[:, f], store_sems.at[f]) for f in range(3)]
    half = RANK // 2
    low = sums[:half]
    lane = lax.broadcasted_iota(jnp.int32, (half, 128), 1)
    upper = jnp.where(lane < RANK, low, 0.0)
    under = jnp.where(lane < RANK, pltpu.roll(low, 128 - RANK, 1), 0.0)
    cross = sums[half : half + 8]
    rest = jnp.zeros((RANK - 8, 128), jnp.float32)
    lane = lax.broadcasted_iota(jnp.int32, (8, 128), 1)
    corner = jnp.where(lane < RANK, 0.0, cross)
    border = jnp.where(lane < RANK, cross, 0.0)
    flat = jnp.zeros((RANK, 128), jnp.float32)
    mirrored = jnp.transpose(jnp.concatenate([flat, border, rest], axis=0), (1, 0))
    gram = jnp.concatenate([upper, under, corner + border, rest], axis=0) + mirrored
    refine(gram * outer[...], start, weights[...], coeffs)

    mix = coeffs[:, : RANK + 8].astype(jnp.bfloat16)

    def mixed(field, first, count):
        done = []
        for h in range(count // 8):
            spot = field * rows + first + 8 * h
            tile = [jnp.concatenate([ref[spot + i] for i in range(8)], axis=1) for ref in (turned, snaps)]
            tile = jnp.concatenate(tile, axis=0)
            total = jnp.dot(mix, tile, preferred_element_type=jnp.float32)
            parts = [total[:, 128 * i : 128 * i + 128].reshape(RANK // 8, 8, 128) for i in range(8)]
            done.append(jnp.stack(crossed(parts), axis=1).reshape(RANK, 8, 128))
        done = done[0] if count == 8 else jnp.concatenate(done, axis=1)
        out[:, field, pl.ds(first, count), :] = done.astype(jnp.bfloat16)

    for field in range(3):

        def pair(index, carry, field=field):
            mixed(field, pl.multiple_of(index * 16, 16), 16)
            return carry

        lax.fori_loop(0, rows // 16, pair, 0, unroll=True)
        if rows % 16:
            mixed(field, rows - 8, 8)
        stores[field].start()
    for store in stores:
        store.wait()


def local(surface, depth, coriolis, land_sea, basis, energies, start):
    rows, cols = depth.shape
    final_state, snaps, turned, gram_base = window(surface, depth, coriolis, land_sea, basis)
    cross = over_cells(snaps, turned)
    square = over_cells(snaps, snaps)
    half = RANK // 2
    sums = jnp.concatenate(
        [
            jnp.concatenate([gram_base[:half], gram_base[half:]], axis=1),
            jnp.pad(jnp.concatenate([cross, square], axis=1), ((0, 0), (0, 128 - RANK - 8))),
        ],
        axis=0,
    )
    sums = total_over_devices(sums)
    cells = 3.0 * rows * cols * lax.axis_size("gx") * lax.axis_size("gy")
    weights = jnp.concatenate([energies, jnp.ones((SNAPS,), jnp.float32)])
    weights = jnp.pad(weights, (0, 128 - KCOLS))
    outer = weights[:, None] * weights[None, :] / cells
    begin = jnp.pad(start.T, ((0, 0), (0, 128 - KCOLS)))
    vmem = pl.BlockSpec(memory_space=pltpu.VMEM)
    projected = pl.pallas_call(
        finish_kernel,
        in_specs=[vmem] * 6,
        out_specs=pl.BlockSpec(memory_space=pl.ANY),
        out_shape=jax.ShapeDtypeStruct(basis.shape, jnp.bfloat16),
        scratch_shapes=[
            pltpu.VMEM(basis.shape, jnp.bfloat16),
            pltpu.VMEM((RANK, 128), jnp.float32),
            pltpu.SemaphoreType.DMA((3,)),
        ],
        compiler_params=pltpu.CompilerParams(vmem_limit_bytes=VMEM_LIMIT),
    )(sums, outer, begin, weights[None, :], snaps, turned)
    return (final_state, projected)


def solution(mesh):
    placed = (
        P(None, "gy", "gx"),
        P("gy", "gx"),
        P("gy", "gx"),
        P("gy", "gx"),
        P(None, None, "gy", "gx"),
        P(),
        P(),
    )
    return jax.shard_map(
        local,
        mesh=mesh,
        in_specs=placed,
        out_specs=(P(None, "gy", "gx"), P(None, None, "gy", "gx")),
        check_vma=False,
    )
```

```python
import jax
import jax.numpy as jnp
from jax import lax
from jax.experimental import pallas as pl
from jax.experimental.pallas import tpu as pltpu
from jax.sharding import PartitionSpec as P

RANK = 64
SNAPS = 4
STEPS = 8
SUBITER = 6
KCOLS = RANK + SNAPS
FIELDS = 6
WIDE = 9
PITCH = 21
HALO = 8
VMEM_LIMIT = 20 * 1024 * 1024


def pack_lane(shape, field):
    lane = lax.broadcasted_iota(jnp.int32, shape, 1)
    return (lane + (WIDE - PITCH * field) % 128) & 127


def pack_kernel(fields, packed):
    total = jnp.zeros(packed.shape, jnp.float32)
    for field in range(FIELDS):
        value = fields[field]
        if field:
            value = pltpu.roll(value, PITCH * field, 1)
        total = jnp.where(pack_lane(packed.shape, field) < 2 * WIDE, value, total)
    packed[...] = total


def crossed(eight):
    eight = list(eight)
    row = lax.broadcasted_iota(jnp.int32, eight[0].shape, 1)
    for step in (4, 2, 1):
        keep = (row & step) == 0
        for i in range(8):
            if i & step == 0:
                low, high = eight[i], eight[i + step]
                eight[i] = jnp.where(keep, low, pltpu.roll(high, step, 1))
                eight[i + step] = jnp.where(keep, pltpu.roll(low, 8 - step, 1), high)
    return eight


def seen_kernel(basis, seen):
    seen[...] = jnp.zeros(seen.shape, jnp.float32)


def rows_of(ref, first):
    return jnp.concatenate([ref[first + i] for i in range(8)], axis=1)


def over_lanes(left, right):
    return lax.dot_general(left, right, (((1,), (1,)), ((), ())), preferred_element_type=jnp.float32)


def combined(first, second, odd):
    west = pack_lane(first.shape, 0) < WIDE
    for field in range(1, FIELDS):
        west = west | (pack_lane(first.shape, field) < WIDE)
    return jnp.where(west == (odd == 0), second, first)


def odd_of(axis):
    return lax.axis_index(axis) & 1


def rows_kernel(fields_low, first_low, second_low, fields_high, first_high, second_high, send_first, send_second):
    odd = odd_of("gx")
    halo_low = combined(first_low[...], second_low[...], odd)
    to_south = [fields_low[field, :HALO] for field in range(FIELDS)]
    to_south += [halo_low[:HALO], fields_low[FIELDS - 1, HALO:], halo_low[HALO:]]
    to_south += [jnp.ones((HALO, 128), jnp.float32)]
    to_north = [fields_high[field] for field in range(FIELDS)]
    to_north += [combined(first_high[...], second_high[...], odd)]
    to_north += [jnp.zeros((HALO, 128), jnp.float32)] * (len(to_south) - len(to_north))
    upper = odd_of("gy") == 1
    for index, (south, north) in enumerate(zip(to_south, to_north)):
        span = slice(index * HALO, (index + 1) * HALO)
        send_first[span, :] = jnp.where(upper, south, north)
        send_second[span, :] = jnp.where(upper, north, south)


def window_kernel(
    fields, first_side, second_side, first_rows, second_rows, *rest
):
    turned, gram, _, state, snaps, sums, height, zonal, merid, statics, frames = rest
    rows = fields.shape[1]
    tall = rows + 2 * HALO
    upper = odd_of("gy") == 1
    from_north = jnp.where(upper, second_rows[...], first_rows[...])
    from_south = jnp.where(upper, first_rows[...], second_rows[...])
    halo = jnp.concatenate(
        [
            from_south[FIELDS * HALO : (FIELDS + 1) * HALO, :],
            combined(first_side[...], second_side[...], odd_of("gx")),
            from_north[FIELDS * HALO : (FIELDS + 1) * HALO, :],
        ],
        axis=0,
    )

    def extended(field, value):
        span = slice(field * HALO, (field + 1) * HALO)
        main = jnp.concatenate([from_south[span, :], value, from_north[span, :]], axis=0)
        side = pltpu.roll(halo, 128 - PITCH * field, 1) if field else halo
        return jnp.concatenate([main, side], axis=1)

    def east(value):
        return pltpu.roll(value, 255, 1)

    def west(value):
        return pltpu.roll(value, 1, 1)

    def north(value):
        return pltpu.roll(value, tall - 1, 0)

    def south(value):
        return pltpu.roll(value, 1, 0)

    values = [fields[field] for field in range(FIELDS)]
    for ref, field in ((height, 0), (zonal, 1), (merid, 2)):
        ref[...] = extended(field, values[field])
    statics[0] = extended(3, values[3])
    wet = extended(4, values[4])
    statics[1] = wet * east(wet)
    statics[2] = wet * north(wet)
    deep = extended(5, values[5])
    statics[3] = 0.5 * (deep + east(deep))
    side = pltpu.roll(from_north[(FIELDS + 2) * HALO : (FIELDS + 3) * HALO, :], 128 - PITCH * 5, 1)
    above = jnp.concatenate([from_north[(FIELDS + 1) * HALO : (FIELDS + 2) * HALO, :], side], axis=1)
    row = lax.broadcasted_iota(jnp.int32, (tall, 256), 0)
    upper = jnp.where(row == tall - 1, above[:1], north(deep))
    statics[4] = 0.5 * (deep + upper)
    there = from_north[(FIELDS + 3) * HALO :, :]
    there = jnp.concatenate([there, there], axis=1)

    def one_step():
        flux = statics[3] * zonal[...]
        drop = statics[4] * merid[...]
        high = height[...] - (flux - west(flux)) - (drop - south(drop))
        high = jnp.concatenate([high[: tall - HALO], high[tall - HALO :] * there], axis=0)
        height[...] = high
        across = merid[...]
        across = across + east(across)
        vbar = 0.25 * (across + south(across))
        flow = statics[1] * (zonal[...] - (east(high) - high) + statics[0] * vbar)
        zonal[...] = flow
        across = flow + west(flow)
        ubar = 0.25 * (across + north(across))
        merid[...] = statics[2] * (merid[...] - (north(high) - high) - statics[0] * ubar)

    def some_steps(turn, carry):
        for _ in range(STEPS // SNAPS):
            one_step()
        for index, ref in enumerate((height, zonal, merid)):
            place = pl.ds(index * rows * 8 + turn, rows, stride=8)
            frames[place, :] = ref[HALO : HALO + rows, :128]
        return carry

    frames[...] = jnp.zeros(frames.shape, jnp.float32)

    lax.fori_loop(0, SNAPS, some_steps, 0)
    for index, ref in enumerate((height, zonal, merid)):
        state[index] = ref[HALO : HALO + rows, :128]
    snaps[...] = frames[...].reshape(snaps.shape).astype(jnp.bfloat16)

    total = jnp.zeros((8, RANK + 8), jnp.float32)
    for field in range(3):
        for first in range(0, rows, 8):
            frame = rows_of(snaps, field * rows + first)
            tile = jnp.concatenate([rows_of(turned, field * rows + first), frame], axis=0)
            total = total + over_lanes(frame, tile)
    pack_sums(gram[...], total, sums)


def triangle(shape):
    row, lane = (lax.broadcasted_iota(jnp.int32, shape, axis) for axis in (0, 1))
    return lane - shape[0] - row, (lane >= shape[0]) & (lane < 2 * shape[0])


def pack_sums(gram, cross, sums):
    half = RANK // 2
    wide = jnp.concatenate([gram, jnp.zeros((RANK, RANK), jnp.float32)], axis=1)
    apart, there = triangle((half, 128))
    first = pltpu.roll(wide[:half], half, 1)
    block = jnp.where(there, jnp.where(apart >= 0, first, wide[half:]), pltpu.roll(first, RANK, 1))
    block = jnp.where(there | (apart < 0), block, 0.0)
    sums[: half // 2, :] = block[: half // 2] + pltpu.roll(block[half // 2 :], RANK, 1)
    diagonal = jnp.sum(jnp.where(there & (apart == 0), wide[half:], 0.0), axis=0, keepdims=True)
    cross = jnp.concatenate([cross, jnp.zeros((8, 128 - RANK - 8), jnp.float32)], axis=1)
    row = lax.broadcasted_iota(jnp.int32, cross.shape, 0)
    sums[half // 2 :, :] = jnp.where(row < SNAPS, cross, jnp.where(row == SNAPS, diagonal, 0.0))


def unpacked(sums):
    half = RANK // 2
    upper = sums[: half // 2]
    block = jnp.concatenate([upper, pltpu.roll(upper, RANK, 1)], axis=0)
    lane = lax.broadcasted_iota(jnp.int32, block.shape, 1)
    apart, there = triangle(block.shape)
    rest = sums[half // 2 :]
    first = jnp.where(there, jnp.where(apart > 0, block, jnp.where(apart == 0, 0.5 * block, 0.0)), 0.0)
    first = pltpu.roll(first, 128 - half, 1) + jnp.where(there, pltpu.roll(block, half, 1), 0.0)
    diagonal = jnp.where(there & (apart == 0), 0.5 * rest[SNAPS : SNAPS + 1], 0.0)
    second = jnp.where(there & (apart < 0), block, diagonal)
    row = lax.broadcasted_iota(jnp.int32, rest.shape, 0)
    lane = lax.broadcasted_iota(jnp.int32, rest.shape, 1)
    third = jnp.where(row < SNAPS, jnp.where(lane < RANK, rest, 0.5 * rest), 0.0)
    third = jnp.where(lane < KCOLS, third, 0.0)
    beyond = jnp.zeros((128 - RANK - 8, 128), jnp.float32)
    matrix = jnp.concatenate([first, second, third, beyond], axis=0)
    return matrix + jnp.transpose(matrix, (1, 0))


def pairs(offset, around):
    partners = [(i, (((i - offset) ^ 1) + offset) % 16) for i in range(16)]
    return [(i, j) for i, j in partners if around or abs(i - j) == 1]


def window(surface, depth, coriolis, land_sea, basis):
    rows, cols = depth.shape
    whole = pltpu.CompilerParams(vmem_limit_bytes=VMEM_LIMIT)
    fields = jnp.pad(surface, ((0, FIELDS - 3), (0, 0), (0, 0)))
    for field, value in ((3, coriolis), (4, land_sea), (5, depth)):
        around = ((field, FIELDS - 1 - field), (0, 0), (0, 0))
        fields = fields + jnp.pad(value[None], around).astype(jnp.float32)
    packed = pl.pallas_call(
        pack_kernel,
        out_shape=jax.ShapeDtypeStruct((rows, cols), jnp.float32),
        compiler_params=whole,
    )(fields)
    basis, packed = lax.optimization_barrier((basis, packed))
    sides = [lax.ppermute(packed, "gx", pairs(offset, True)) for offset in (0, 1)]

    seen = pl.pallas_call(
        seen_kernel,
        in_specs=[pl.BlockSpec(memory_space=pl.ANY)],
        out_shape=jax.ShapeDtypeStruct((HALO, cols), jnp.float32),
        compiler_params=whole,
    )(basis)
    seen, sides = lax.optimization_barrier((seen, sides))

    def strips(height, index):
        side = pl.BlockSpec((height, cols), lambda i: (index, 0))
        return [pl.BlockSpec((FIELDS, height, cols), lambda i: (0, index, 0)), side, side]

    slab = jax.ShapeDtypeStruct(((FIELDS + 4) * HALO, cols), jnp.float32)
    sends = pl.pallas_call(
        rows_kernel,
        grid=(1,),
        in_specs=strips(2 * HALO, 0) + strips(HALO, rows // HALO - 1),
        out_shape=(slab, slab),
        compiler_params=whole,
    )(fields, *sides, fields, *sides)
    slabs = [lax.ppermute(send, "gy", pairs(offset, False)) for offset, send in enumerate(sends)]
    basis, slabs[0], seen = lax.optimization_barrier((basis, slabs[0], seen))
    turned = jnp.transpose(basis, (1, 2, 0, 3)).reshape(3 * rows, RANK, cols)
    turned = lax.optimization_barrier(turned)
    gram = lax.dot_general(
        turned, turned, (((0, 2), (0, 2)), ((), ())), preferred_element_type=jnp.float32
    )
    gram, slabs = lax.optimization_barrier((gram, slabs))
    tall = (rows + 2 * HALO, 2 * cols)
    final_state, snaps, sums = pl.pallas_call(
        window_kernel,
        out_shape=(
            jax.ShapeDtypeStruct((3, rows, cols), jnp.float32),
            jax.ShapeDtypeStruct((3 * rows, 8, cols), jnp.bfloat16),
            jax.ShapeDtypeStruct((RANK // 4 + 8, 128), jnp.float32),
        ),
        scratch_shapes=[pltpu.VMEM(tall, jnp.float32)] * 3
        + [pltpu.VMEM((5,) + tall, jnp.float32), pltpu.VMEM((3 * rows * 8, cols), jnp.float32)],
        compiler_params=whole,
    )(fields, *sides, *slabs, turned, gram, seen)
    return final_state, snaps, turned, sums


def exchanged(value, axis, partner):
    return lax.ppermute(value, axis, [(i, partner(i)) for i in range(16)])


def quad_sum(value, axis, one, two):
    first = exchanged(value, axis, lambda i: i ^ one)
    second = exchanged(value, axis, lambda i: i ^ two)
    third = exchanged(value, axis, lambda i: i ^ one ^ two)
    return (value + first) + (second + third)


def total_over_devices(value):
    value = quad_sum(value, "gy", 1, 2)
    ring = lambda a: ((a - 1) ^ 1) + 1 if 0 < a < 7 else 7 - a
    value = value + exchanged(value, "gy", lambda i: ring(i // 2) * 2 + i % 2)
    ring = lambda a: (7 - a) if a in (1, 2, 5, 6) else {0: 3, 3: 0, 4: 7, 7: 4}[a]
    value = value + exchanged(value, "gy", lambda i: ring(i // 2) * 2 + i % 2)
    value = quad_sum(value, "gx", 1, 4)
    return quad_sum(value, "gx", 3, 12)


ORDERS = ((0, 0), (0, 1), (1, 0), (0, 2), (1, 1), (2, 0))
PITCH_OF_SWEEP = 176
LEAD = 56


def parts_of(value):
    parts = []
    for _ in range(3):
        parts.append(value.astype(jnp.bfloat16))
        value = value - parts[-1].astype(jnp.float32)
    return parts


def parts_dot(left, right, count, turned=False):
    left = jnp.concatenate([left[i] for i, _ in ORDERS[:count]], axis=1)
    right = jnp.concatenate([right[j] for _, j in ORDERS[:count]], axis=1 if turned else 0)
    return lax.dot_general(
        left, right, (((1,), (1 if turned else 0,)), ((), ())), preferred_element_type=jnp.float32
    )


def refine(gram, start, weights, store):
    blocks = RANK // 8
    sweep = lax.broadcasted_iota(jnp.int32, (8, 128), 0)
    gram = parts_of(gram)
    made = None
    for time in range(blocks + SUBITER - 1):
        inputs = []
        for i in range(8):
            value = jnp.zeros((8, 128), jnp.float32) if made is None else pltpu.roll(made[i], 1, 0)
            if time < blocks:
                value = jnp.where(sweep == 0, start[8 * time + i : 8 * time + i + 1, :], value)
            inputs.append(value)
        active = (sweep <= time) & (sweep > time - blocks) & (sweep < SUBITER)
        images = parts_dot(parts_of(jnp.concatenate(inputs, axis=0)), gram, 6)
        running = [k for k in range(SUBITER) if 0 < time - k < blocks]
        if running:
            history = [store[pl.ds(k * PITCH_OF_SWEEP + LEAD, 8 * (time - k)), :] for k in running]
            length = sum(rows.shape[0] for rows in history)
            if length % 128:
                history.append(jnp.zeros((128 - length % 128, 128), jnp.float32))
            history = parts_of(jnp.concatenate(history, axis=0))
            inner = parts_dot(parts_of(images), history, 3, turned=True)
            row = lax.broadcasted_iota(jnp.int32, inner.shape, 0) & 7
            col = lax.broadcasted_iota(jnp.int32, inner.shape, 1)
            owner, edge = jnp.full(inner.shape, running[0], jnp.int32), 0
            for k in running[:-1]:
                edge += 8 * (time - k)
                owner = owner + jnp.where(col >= edge, 1, 0)
            inner = jnp.where(row == owner, inner, 0.0)
            images = images - parts_dot(parts_of(inner), history, 5)
        parts = [images[8 * i : 8 * i + 8] for i in range(8)]
        square = {
            (i, j): jnp.sum(parts[i] * parts[j], axis=1, keepdims=True)
            for i in range(8)
            for j in range(i, 8)
        }
        made = []
        for i in range(8):
            scale = lax.rsqrt(square[i, i])
            unit = parts[i] * scale
            made.append(jnp.where(active, unit, 0.0))
            lower = {j: square[i, j] * scale for j in range(i + 1, 8)}
            for j in range(i + 1, 8):
                parts[j] = parts[j] - lower[j] * unit
                for p in range(j, 8):
                    square[j, p] = square[j, p] - lower[j] * lower[p]
        for i in range(8):
            store[pl.ds(LEAD + 8 * time + i, 8, stride=PITCH_OF_SWEEP - 8), :] = made[i]
    return store[pl.ds((SUBITER - 1) * PITCH_OF_SWEEP + LEAD, RANK), :] * weights


def finish_kernel(
    sums, outer, start, weights, snaps, turned, projected, out, store, store_sems
):
    rows = out.shape[2]
    stores = [pltpu.make_async_copy(out.at[:, f], projected.at[:, f], store_sems.at[f]) for f in range(3)]
    gram = unpacked(sums[...])
    coeffs = refine(gram * outer[...], start, weights[...], store)

    mix = coeffs[:, : RANK + 8].astype(jnp.bfloat16)

    def mixed(field, first, count):
        done = []
        for h in range(count // 8):
            spot = field * rows + first + 8 * h
            tile = jnp.concatenate([rows_of(turned, spot), rows_of(snaps, spot)], axis=0)
            total = jnp.dot(mix, tile, preferred_element_type=jnp.float32)
            parts = [total[:, 128 * i : 128 * i + 128].reshape(RANK // 8, 8, 128) for i in range(8)]
            done.append(jnp.stack(crossed(parts), axis=1).reshape(RANK, 8, 128))
        done = done[0] if count == 8 else jnp.concatenate(done, axis=1)
        out[:, field, pl.ds(first, count), :] = done.astype(jnp.bfloat16)

    for field in range(3):

        def pair(index, carry, field=field):
            mixed(field, pl.multiple_of(index * 16, 16), 16)
            return carry

        lax.fori_loop(0, rows // 16, pair, 0, unroll=True)
        if rows % 16:
            mixed(field, rows - 8, 8)
        stores[field].start()
    for store in stores:
        store.wait()


def local(surface, depth, coriolis, land_sea, basis, energies, start):
    rows, cols = depth.shape
    final_state, snaps, turned, sums = window(surface, depth, coriolis, land_sea, basis)
    sums = total_over_devices(sums)
    cells = 3.0 * rows * cols * lax.axis_size("gx") * lax.axis_size("gy")
    weights = jnp.concatenate([energies, jnp.ones((SNAPS,), jnp.float32)])
    weights = jnp.pad(weights, (0, 128 - KCOLS))
    outer = weights[:, None] * weights[None, :] / cells
    begin = jnp.pad(start.T, ((0, 0), (0, 128 - KCOLS)))
    vmem = pl.BlockSpec(memory_space=pltpu.VMEM)
    projected = pl.pallas_call(
        finish_kernel,
        in_specs=[vmem] * 6,
        out_specs=pl.BlockSpec(memory_space=pl.ANY),
        out_shape=jax.ShapeDtypeStruct(basis.shape, jnp.bfloat16),
        scratch_shapes=[
            pltpu.VMEM(basis.shape, jnp.bfloat16),
            pltpu.VMEM((8 * PITCH_OF_SWEEP, 128), jnp.float32),
            pltpu.SemaphoreType.DMA((3,)),
        ],
        compiler_params=pltpu.CompilerParams(vmem_limit_bytes=VMEM_LIMIT),
    )(sums, outer, begin, weights[None, :], snaps, turned)
    return (final_state, projected)


def solution(mesh):
    placed = (
        P(None, "gy", "gx"),
        P("gy", "gx"),
        P("gy", "gx"),
        P("gy", "gx"),
        P(None, None, "gy", "gx"),
        P(),
        P(),
    )
    return jax.shard_map(
        local,
        mesh=mesh,
        in_specs=placed,
        out_specs=(P(None, "gy", "gx"), P(None, None, "gy", "gx")),
        check_vma=False,
    )
```

```python
import jax
import jax.numpy as jnp
from jax import lax
from jax.experimental import pallas as pl
from jax.experimental.pallas import tpu as pltpu
from jax.sharding import PartitionSpec as P

RANK = 64
SNAPS = 4
STEPS = 8
SUBITER = 6
KCOLS = RANK + SNAPS
FIELDS = 6
WIDE = 9
PITCH = 21
HALO = 8
VMEM_LIMIT = 20 * 1024 * 1024


def pack_lane(shape, field):
    lane = lax.broadcasted_iota(jnp.int32, shape, 1)
    return (lane + (WIDE - PITCH * field) % 128) & 127


def pack_kernel(fields, packed):
    total = jnp.zeros(packed.shape, jnp.float32)
    for field in range(FIELDS):
        value = fields[field]
        if field:
            value = pltpu.roll(value, PITCH * field, 1)
        total = jnp.where(pack_lane(packed.shape, field) < 2 * WIDE, value, total)
    packed[...] = total


def crossed(eight):
    eight = list(eight)
    row = lax.broadcasted_iota(jnp.int32, eight[0].shape, 1)
    for step in (4, 2, 1):
        keep = (row & step) == 0
        for i in range(8):
            if i & step == 0:
                low, high = eight[i], eight[i + step]
                eight[i] = jnp.where(keep, low, pltpu.roll(high, step, 1))
                eight[i + step] = jnp.where(keep, pltpu.roll(low, 8 - step, 1), high)
    return eight


def seen_kernel(value, seen):
    seen[...] = jnp.zeros(seen.shape, jnp.float32)


def seen_by_kernel(value, limit=VMEM_LIMIT):
    return pl.pallas_call(
        seen_kernel,
        in_specs=[pl.BlockSpec(memory_space=pl.ANY)],
        out_shape=jax.ShapeDtypeStruct((HALO, 128), jnp.float32),
        compiler_params=pltpu.CompilerParams(vmem_limit_bytes=limit),
    )(value)


def rows_of(ref, first):
    return jnp.concatenate([ref[first + i] for i in range(8)], axis=1)


def over_lanes(left, right):
    return lax.dot_general(left, right, (((1,), (1,)), ((), ())), preferred_element_type=jnp.float32)


def combined(first, second, odd):
    west = pack_lane(first.shape, 0) < WIDE
    for field in range(1, FIELDS):
        west = west | (pack_lane(first.shape, field) < WIDE)
    return jnp.where(west == (odd == 0), second, first)


def odd_of(axis):
    return lax.axis_index(axis) & 1


def rows_kernel(fields_low, first_low, second_low, fields_high, first_high, second_high, send_first, send_second):
    odd = odd_of("gx")
    halo_low = combined(first_low[...], second_low[...], odd)
    to_south = [fields_low[field, :HALO] for field in range(FIELDS)]
    to_south += [halo_low[:HALO], fields_low[FIELDS - 1, HALO:], halo_low[HALO:]]
    to_south += [jnp.ones((HALO, 128), jnp.float32)]
    to_north = [fields_high[field] for field in range(FIELDS)]
    to_north += [combined(first_high[...], second_high[...], odd)]
    to_north += [jnp.zeros((HALO, 128), jnp.float32)] * (len(to_south) - len(to_north))
    upper = odd_of("gy") == 1
    for index, (south, north) in enumerate(zip(to_south, to_north)):
        span = slice(index * HALO, (index + 1) * HALO)
        send_first[span, :] = jnp.where(upper, south, north)
        send_second[span, :] = jnp.where(upper, north, south)


def window_kernel(
    fields, first_side, second_side, first_rows, second_rows, *rest
):
    turned, gram, _, _, state, snaps, sums, height, zonal, merid, statics, frames = rest
    rows = fields.shape[1]
    tall = rows + 2 * HALO
    upper = odd_of("gy") == 1
    from_north = jnp.where(upper, second_rows[...], first_rows[...])
    from_south = jnp.where(upper, first_rows[...], second_rows[...])
    halo = jnp.concatenate(
        [
            from_south[FIELDS * HALO : (FIELDS + 1) * HALO, :],
            combined(first_side[...], second_side[...], odd_of("gx")),
            from_north[FIELDS * HALO : (FIELDS + 1) * HALO, :],
        ],
        axis=0,
    )

    def extended(field, value):
        span = slice(field * HALO, (field + 1) * HALO)
        main = jnp.concatenate([from_south[span, :], value, from_north[span, :]], axis=0)
        side = pltpu.roll(halo, 128 - PITCH * field, 1) if field else halo
        return jnp.concatenate([main, side], axis=1)

    def east(value):
        return pltpu.roll(value, 255, 1)

    def west(value):
        return pltpu.roll(value, 1, 1)

    def north(value):
        return pltpu.roll(value, tall - 1, 0)

    values = [fields[field] for field in range(FIELDS)]
    for ref, field in ((height, 0), (zonal, 1), (merid, 2)):
        ref[...] = extended(field, values[field])
    statics[0] = extended(3, values[3])
    wet = extended(4, values[4])
    statics[1] = wet * east(wet)
    statics[2] = wet * north(wet)
    deep = extended(5, values[5])
    statics[3] = 0.5 * (deep + east(deep))
    side = pltpu.roll(from_north[(FIELDS + 2) * HALO : (FIELDS + 3) * HALO, :], 128 - PITCH * 5, 1)
    above = jnp.concatenate([from_north[(FIELDS + 1) * HALO : (FIELDS + 2) * HALO, :], side], axis=1)
    last = lax.broadcasted_iota(jnp.int32, (tall, 256), 0) == tall - 1
    upper = jnp.where(last, above[:1], north(deep))
    statics[4] = 0.5 * (deep + upper)
    there = from_north[(FIELDS + 3) * HALO :, :]
    there = jnp.concatenate([there, there], axis=1)
    row = lax.broadcasted_iota(jnp.int32, (8, 256), 0)

    def one_step():
        def shifted_south(value, below):
            return jnp.where(row == 0, pltpu.roll(below, 1, 0), pltpu.roll(value, 1, 0))

        def shifted_north(value, above):
            return jnp.where(row == 7, pltpu.roll(above, 7, 0), pltpu.roll(value, 7, 0))

        before = None
        for first in range(0, tall, 8):
            span = slice(first, first + 8)
            flow, across = zonal[span, :], merid[span, :]
            flux = statics[3, span, :] * flow
            drop = statics[4, span, :] * across
            sums = across + east(across)
            low = before or dict(drop=drop, sums=sums)
            high = height[span, :] - (flux - west(flux)) - (drop - shifted_south(drop, low["drop"]))
            if first == tall - HALO:
                high = high * there
            vbar = 0.25 * (sums + shifted_south(sums, low["sums"]))
            flow = statics[1, span, :] * (flow - (east(high) - high) + statics[0, span, :] * vbar)
            height[span, :] = high
            zonal[span, :] = flow
            now = dict(drop=drop, sums=sums, high=high, pairs=flow + west(flow), across=across, span=span)
            if before:
                finish_merid(before, now["high"], now["pairs"], shifted_north)
            before = now
        finish_merid(before, before["high"], before["pairs"], shifted_north)

    def finish_merid(rows_here, high_above, pairs_above, shifted_north):
        high, pairs_here, span = rows_here["high"], rows_here["pairs"], rows_here["span"]
        ubar = 0.25 * (pairs_here + shifted_north(pairs_here, pairs_above))
        slope = shifted_north(high, high_above) - high
        merid[span, :] = statics[2, span, :] * (rows_here["across"] - slope - statics[0, span, :] * ubar)

    def some_steps(turn, carry):
        for _ in range(STEPS // SNAPS):
            one_step()
        for index, ref in enumerate((height, zonal, merid)):
            place = pl.ds(index * rows * 8 + turn, rows, stride=8)
            frames[place, :] = ref[HALO : HALO + rows, :128]
        return carry

    frames[...] = jnp.zeros(frames.shape, jnp.float32)

    lax.fori_loop(0, SNAPS, some_steps, 0)
    for index, ref in enumerate((height, zonal, merid)):
        state[index] = ref[HALO : HALO + rows, :128]
    snaps[...] = frames[...].reshape(snaps.shape).astype(jnp.bfloat16)

    total = jnp.zeros((8, RANK + 8), jnp.float32)
    for field in range(3):
        for first in range(0, rows, 8):
            frame = rows_of(snaps, field * rows + first)
            tile = jnp.concatenate([rows_of(turned, field * rows + first), frame], axis=0)
            total = total + over_lanes(frame, tile)
    pack_sums(gram[...], total, sums)


def triangle(shape):
    row, lane = (lax.broadcasted_iota(jnp.int32, shape, axis) for axis in (0, 1))
    return lane - shape[0] - row, (lane >= shape[0]) & (lane < 2 * shape[0])


def pack_sums(gram, cross, sums):
    half = RANK // 2
    wide = jnp.concatenate([gram, jnp.zeros((RANK, RANK), jnp.float32)], axis=1)
    apart, there = triangle((half, 128))
    first = pltpu.roll(wide[:half], half, 1)
    block = jnp.where(there, jnp.where(apart >= 0, first, wide[half:]), pltpu.roll(first, RANK, 1))
    block = jnp.where(there | (apart < 0), block, 0.0)
    sums[: half // 2, :] = block[: half // 2] + pltpu.roll(block[half // 2 :], RANK, 1)
    diagonal = jnp.sum(jnp.where(there & (apart == 0), wide[half:], 0.0), axis=0, keepdims=True)
    cross = jnp.concatenate([cross, jnp.zeros((8, 128 - RANK - 8), jnp.float32)], axis=1)
    row = lax.broadcasted_iota(jnp.int32, cross.shape, 0)
    sums[half // 2 :, :] = jnp.where(row < SNAPS, cross, jnp.where(row == SNAPS, diagonal, 0.0))


def unpacked(sums):
    half = RANK // 2
    upper = sums[: half // 2]
    block = jnp.concatenate([upper, pltpu.roll(upper, RANK, 1)], axis=0)
    lane = lax.broadcasted_iota(jnp.int32, block.shape, 1)
    apart, there = triangle(block.shape)
    rest = sums[half // 2 :]
    first = jnp.where(there, jnp.where(apart > 0, block, jnp.where(apart == 0, 0.5 * block, 0.0)), 0.0)
    first = pltpu.roll(first, 128 - half, 1) + jnp.where(there, pltpu.roll(block, half, 1), 0.0)
    diagonal = jnp.where(there & (apart == 0), 0.5 * rest[SNAPS : SNAPS + 1], 0.0)
    second = jnp.where(there & (apart < 0), block, diagonal)
    row = lax.broadcasted_iota(jnp.int32, rest.shape, 0)
    lane = lax.broadcasted_iota(jnp.int32, rest.shape, 1)
    third = jnp.where(row < SNAPS, jnp.where(lane < RANK, rest, 0.5 * rest), 0.0)
    third = jnp.where(lane < KCOLS, third, 0.0)
    beyond = jnp.zeros((128 - RANK - 8, 128), jnp.float32)
    matrix = jnp.concatenate([first, second, third, beyond], axis=0)
    return matrix + jnp.transpose(matrix, (1, 0))


def pairs(offset, around):
    partners = [(i, (((i - offset) ^ 1) + offset) % 16) for i in range(16)]
    return [(i, j) for i, j in partners if around or abs(i - j) == 1]


def window(surface, depth, coriolis, land_sea, basis):
    rows, cols = depth.shape
    whole = pltpu.CompilerParams(vmem_limit_bytes=VMEM_LIMIT)
    fields = jnp.pad(surface, ((0, FIELDS - 3), (0, 0), (0, 0)))
    for field, value in ((3, coriolis), (4, land_sea), (5, depth)):
        around = ((field, FIELDS - 1 - field), (0, 0), (0, 0))
        fields = fields + jnp.pad(value[None], around).astype(jnp.float32)
    packed = pl.pallas_call(
        pack_kernel,
        out_shape=jax.ShapeDtypeStruct((rows, cols), jnp.float32),
        compiler_params=whole,
    )(fields)
    basis, packed = lax.optimization_barrier((basis, packed))
    sides = [lax.ppermute(packed, "gx", pairs(offset, True)) for offset in (0, 1)]

    early = seen_by_kernel(basis, 55 * 1024 * 1024)
    early, sides[0] = lax.optimization_barrier((early, sides[0]))
    basis, early = lax.optimization_barrier((basis, early))
    late = seen_by_kernel(basis)
    basis, late = lax.optimization_barrier((basis, late))
    turned = jnp.transpose(basis, (1, 2, 0, 3)).reshape(3 * rows, RANK, cols)
    turned, sides[1], late = lax.optimization_barrier((turned, sides[1], late))

    def strips(height, index):
        side = pl.BlockSpec((height, cols), lambda i: (index, 0))
        return [pl.BlockSpec((FIELDS, height, cols), lambda i: (0, index, 0)), side, side]

    slab = jax.ShapeDtypeStruct(((FIELDS + 4) * HALO, cols), jnp.float32)
    sends = pl.pallas_call(
        rows_kernel,
        grid=(1,),
        in_specs=strips(2 * HALO, 0) + strips(HALO, rows // HALO - 1),
        out_shape=(slab, slab),
        compiler_params=whole,
    )(fields, *sides, fields, *sides)
    slabs = [lax.ppermute(send, "gy", pairs(offset, False)) for offset, send in enumerate(sends)]
    turned, slabs[0] = lax.optimization_barrier((turned, slabs[0]))
    gram = lax.dot_general(
        turned, turned, (((0, 2), (0, 2)), ((), ())), preferred_element_type=jnp.float32
    )
    gram, slabs = lax.optimization_barrier((gram, slabs))
    tall = (rows + 2 * HALO, 2 * cols)
    final_state, snaps, sums = pl.pallas_call(
        window_kernel,
        out_shape=(
            jax.ShapeDtypeStruct((3, rows, cols), jnp.float32),
            jax.ShapeDtypeStruct((3 * rows, 8, cols), jnp.bfloat16),
            jax.ShapeDtypeStruct((RANK // 4 + 8, 128), jnp.float32),
        ),
        scratch_shapes=[pltpu.VMEM(tall, jnp.float32)] * 3
        + [pltpu.VMEM((5,) + tall, jnp.float32), pltpu.VMEM((3 * rows * 8, cols), jnp.float32)],
        compiler_params=whole,
    )(fields, *sides, *slabs, turned, gram, early, late)
    return final_state, snaps, turned, sums


def exchanged(value, axis, partner):
    return lax.ppermute(value, axis, [(i, partner(i)) for i in range(16)])


def quad_sum(value, axis, one, two):
    first = exchanged(value, axis, lambda i: i ^ one)
    second = exchanged(value, axis, lambda i: i ^ two)
    third = exchanged(value, axis, lambda i: i ^ one ^ two)
    return (value + first) + (second + third)


def total_over_devices(value):
    value = quad_sum(value, "gy", 1, 2)
    ring = lambda a: ((a - 1) ^ 1) + 1 if 0 < a < 7 else 7 - a
    value = value + exchanged(value, "gy", lambda i: ring(i // 2) * 2 + i % 2)
    ring = lambda a: (7 - a) if a in (1, 2, 5, 6) else {0: 3, 3: 0, 4: 7, 7: 4}[a]
    value = value + exchanged(value, "gy", lambda i: ring(i // 2) * 2 + i % 2)
    value = quad_sum(value, "gx", 1, 4)
    return quad_sum(value, "gx", 3, 12)


ORDERS = ((0, 0), (0, 1), (1, 0), (0, 2), (1, 1), (2, 0))
PITCH_OF_SWEEP = 176
LEAD = 56
GROUPS = ((0, 32), (32, 32))


def parts_of(value):
    parts = []
    for _ in range(3):
        parts.append(value.astype(jnp.bfloat16))
        value = value - parts[-1].astype(jnp.float32)
    return parts


def parts_dot(left, right, count, turned=False):
    left = jnp.concatenate([left[i] for i, _ in ORDERS[:count]], axis=1)
    right = jnp.concatenate([right[j] for _, j in ORDERS[:count]], axis=1 if turned else 0)
    return lax.dot_general(
        left, right, (((1,), (1 if turned else 0,)), ((), ())), preferred_element_type=jnp.float32
    )


def refine(gram, start, store):
    blocks = RANK // 8
    sweep = lax.broadcasted_iota(jnp.int32, (8, 128), 0)
    gram = parts_of(gram)
    made = None
    for time in range(blocks + SUBITER - 1):
        inputs = []
        for i in range(8):
            value = jnp.zeros((8, 128), jnp.float32) if made is None else pltpu.roll(made[i], 1, 0)
            if time < blocks:
                value = jnp.where(sweep == 0, start[8 * time + i : 8 * time + i + 1, :], value)
            inputs.append(value)
        active = (sweep <= time) & (sweep > time - blocks) & (sweep < SUBITER)
        images = parts_dot(parts_of(jnp.concatenate(inputs, axis=0)), gram, 6)
        running = [k for k in range(SUBITER) if 0 < time - k < blocks]
        if running:
            history = [store[pl.ds(k * PITCH_OF_SWEEP + LEAD, 8 * (time - k)), :] for k in running]
            length = sum(rows.shape[0] for rows in history)
            if length % 128:
                history.append(jnp.zeros((128 - length % 128, 128), jnp.float32))
            history = parts_of(jnp.concatenate(history, axis=0))
            inner = parts_dot(parts_of(images), history, 3, turned=True)
            row = lax.broadcasted_iota(jnp.int32, inner.shape, 0) & 7
            col = lax.broadcasted_iota(jnp.int32, inner.shape, 1)
            owner, edge = jnp.full(inner.shape, running[0], jnp.int32), 0
            for k in running[:-1]:
                edge += 8 * (time - k)
                owner = owner + jnp.where(col >= edge, 1, 0)
            inner = jnp.where(row == owner, inner, 0.0)
            images = images - parts_dot(parts_of(inner), history, 5)
        parts = [images[8 * i : 8 * i + 8] for i in range(8)]
        square = {
            (i, j): jnp.sum(parts[i] * parts[j], axis=1, keepdims=True)
            for i in range(8)
            for j in range(i, 8)
        }
        made = []
        for i in range(8):
            scale = lax.rsqrt(square[i, i])
            unit = parts[i] * scale
            made.append(jnp.where(active, unit, 0.0))
            lower = {j: square[i, j] * scale for j in range(i + 1, 8)}
            for j in range(i + 1, 8):
                parts[j] = parts[j] - lower[j] * unit
                for p in range(j, 8):
                    square[j, p] = square[j, p] - lower[j] * lower[p]
        for i in range(8):
            store[pl.ds(LEAD + 8 * time + i, 8, stride=PITCH_OF_SWEEP - 8), :] = made[i]
        yield time


def finish_kernel(
    sums, outer, start, weights, snaps, turned, projected, out, store, store_sems
):
    rows = out.shape[2]
    stores = [
        [
            pltpu.make_async_copy(
                out.at[pl.ds(first, size), f], projected.at[pl.ds(first, size), f], store_sems.at[3 * index + f]
            )
            for f in range(3)
        ]
        for index, (first, size) in enumerate(GROUPS)
    ]
    bands = [(f, first, min(16, rows - first)) for f in range(3) for first in range(0, rows, 16)]
    gram = unpacked(sums[...])

    def mix_of(index):
        first, size = GROUPS[index]
        rows_of_mix = store[pl.ds((SUBITER - 1) * PITCH_OF_SWEEP + LEAD + first, size), :] * weights[...]
        return rows_of_mix[:, : RANK + 8].astype(jnp.bfloat16)

    def mixed(index, mix, field, first, count):
        made, size = GROUPS[index]
        done = []
        for h in range(count // 8):
            spot = field * rows + first + 8 * h
            tile = jnp.concatenate([rows_of(turned, spot), rows_of(snaps, spot)], axis=0)
            total = jnp.dot(mix, tile, preferred_element_type=jnp.float32)
            parts = [total[:, 128 * i : 128 * i + 128].reshape(size // 8, 8, 128) for i in range(8)]
            done.append(jnp.stack(crossed(parts), axis=1).reshape(size, 8, 128))
        done = done[0] if count == 8 else jnp.concatenate(done, axis=1)
        out[made : made + size, field, first : first + count, :] = done.astype(jnp.bfloat16)
        if first + count == rows:
            stores[index][field].start()

    last = RANK // 8 + SUBITER - 2
    ready = [SUBITER - 2 + (first + size) // 8 for first, size in GROUPS]
    work = []
    for time in refine(gram * outer[...], start, store):
        for index, due in enumerate(ready):
            if time == due:
                mix = mix_of(index)
                work += [(index, mix, *band) for band in bands]
        if time < last:
            until = min([due for due in ready if due > time])
            now = -(-len(work) // (until - time))
            for item in work[:now]:
                mixed(*item)
            work = work[now:]
    for item in work:
        mixed(*item)
    for group in stores:
        for copy in group:
            copy.wait()


def local(surface, depth, coriolis, land_sea, basis, energies, start):
    rows, cols = depth.shape
    final_state, snaps, turned, sums = window(surface, depth, coriolis, land_sea, basis)
    sums = total_over_devices(sums)
    cells = 3.0 * rows * cols * lax.axis_size("gx") * lax.axis_size("gy")
    weights = jnp.concatenate([energies, jnp.ones((SNAPS,), jnp.float32)])
    weights = jnp.pad(weights, (0, 128 - KCOLS))
    outer = weights[:, None] * weights[None, :] / cells
    begin = jnp.pad(start.T, ((0, 0), (0, 128 - KCOLS)))
    vmem = pl.BlockSpec(memory_space=pltpu.VMEM)
    projected = pl.pallas_call(
        finish_kernel,
        in_specs=[vmem] * 6,
        out_specs=pl.BlockSpec(memory_space=pl.ANY),
        out_shape=jax.ShapeDtypeStruct(basis.shape, jnp.bfloat16),
        scratch_shapes=[
            pltpu.VMEM(basis.shape, jnp.bfloat16),
            pltpu.VMEM((8 * PITCH_OF_SWEEP, 128), jnp.float32),
            pltpu.SemaphoreType.DMA((3 * len(GROUPS),)),
        ],
        compiler_params=pltpu.CompilerParams(vmem_limit_bytes=VMEM_LIMIT),
    )(sums, outer, begin, weights[None, :], snaps, turned)
    return (final_state, projected)


def solution(mesh):
    placed = (
        P(None, "gy", "gx"),
        P("gy", "gx"),
        P("gy", "gx"),
        P("gy", "gx"),
        P(None, None, "gy", "gx"),
        P(),
        P(),
    )
    return jax.shard_map(
        local,
        mesh=mesh,
        in_specs=placed,
        out_specs=(P(None, "gy", "gx"), P(None, None, "gy", "gx")),
        check_vma=False,
    )
```

```python
import jax
import jax.numpy as jnp
from jax import lax
from jax.experimental import pallas as pl
from jax.experimental.pallas import tpu as pltpu
from jax.sharding import PartitionSpec as P

RANK = 64
SNAPS = 4
STEPS = 8
SUBITER = 6
KCOLS = RANK + SNAPS
FIELDS = 6
WIDE = 9
PITCH = 21
HALO = 8
VMEM_LIMIT = 20 * 1024 * 1024


def pack_lane(shape, field):
    lane = lax.broadcasted_iota(jnp.int32, shape, 1)
    return (lane + (WIDE - PITCH * field) % 128) & 127


def pack_kernel(fields, packed):
    total = jnp.zeros(packed.shape, jnp.float32)
    for field in range(FIELDS):
        value = fields[field]
        if field:
            value = pltpu.roll(value, PITCH * field, 1)
        total = jnp.where(pack_lane(packed.shape, field) < 2 * WIDE, value, total)
    packed[...] = total


def crossed(eight):
    eight = list(eight)
    row = lax.broadcasted_iota(jnp.int32, eight[0].shape, 1)
    for step in (4, 2, 1):
        keep = (row & step) == 0
        for i in range(8):
            if i & step == 0:
                low, high = eight[i], eight[i + step]
                eight[i] = jnp.where(keep, low, pltpu.roll(high, step, 1))
                eight[i + step] = jnp.where(keep, pltpu.roll(low, 8 - step, 1), high)
    return eight


def seen_kernel(value, seen):
    seen[...] = jnp.zeros(seen.shape, jnp.float32)


def seen_by_kernel(value, limit=VMEM_LIMIT):
    return pl.pallas_call(
        seen_kernel,
        in_specs=[pl.BlockSpec(memory_space=pl.ANY)],
        out_shape=jax.ShapeDtypeStruct((HALO, 128), jnp.float32),
        compiler_params=pltpu.CompilerParams(vmem_limit_bytes=limit),
    )(value)


def rows_of(ref, first):
    return jnp.concatenate([ref[first + i] for i in range(8)], axis=1)


def over_lanes(left, right):
    return lax.dot_general(left, right, (((1,), (1,)), ((), ())), preferred_element_type=jnp.float32)


def combined(first, second, odd):
    west = pack_lane(first.shape, 0) < WIDE
    for field in range(1, FIELDS):
        west = west | (pack_lane(first.shape, field) < WIDE)
    return jnp.where(west == (odd == 0), second, first)


def odd_of(axis):
    return lax.axis_index(axis) & 1


def rows_kernel(fields_low, first_low, second_low, fields_high, first_high, second_high, send_first, send_second):
    odd = odd_of("gx")
    halo_low = combined(first_low[...], second_low[...], odd)
    to_south = [fields_low[field, :HALO] for field in range(FIELDS)]
    to_south += [halo_low[:HALO], fields_low[FIELDS - 1, HALO:], halo_low[HALO:]]
    to_south += [jnp.ones((HALO, 128), jnp.float32)]
    to_north = [fields_high[field] for field in range(FIELDS)]
    to_north += [combined(first_high[...], second_high[...], odd)]
    to_north += [jnp.zeros((HALO, 128), jnp.float32)] * (len(to_south) - len(to_north))
    upper = odd_of("gy") == 1
    for index, (south, north) in enumerate(zip(to_south, to_north)):
        span = slice(index * HALO, (index + 1) * HALO)
        send_first[span, :] = jnp.where(upper, south, north)
        send_second[span, :] = jnp.where(upper, north, south)


def window_kernel(
    fields, first_side, second_side, first_rows, second_rows, *rest
):
    turned, gram, _, _, state, snaps, sums, height, zonal, merid, statics, frames = rest
    rows = fields.shape[1]
    tall = rows + 2 * HALO
    upper = odd_of("gy") == 1
    from_north = jnp.where(upper, second_rows[...], first_rows[...])
    from_south = jnp.where(upper, first_rows[...], second_rows[...])
    halo = jnp.concatenate(
        [
            from_south[FIELDS * HALO : (FIELDS + 1) * HALO, :],
            combined(first_side[...], second_side[...], odd_of("gx")),
            from_north[FIELDS * HALO : (FIELDS + 1) * HALO, :],
        ],
        axis=0,
    )

    def extended(field, value):
        span = slice(field * HALO, (field + 1) * HALO)
        main = jnp.concatenate([from_south[span, :], value, from_north[span, :]], axis=0)
        side = pltpu.roll(halo, 128 - PITCH * field, 1) if field else halo
        return jnp.concatenate([main, side], axis=1)

    def east(value):
        return pltpu.roll(value, 255, 1)

    def west(value):
        return pltpu.roll(value, 1, 1)

    def north(value):
        return pltpu.roll(value, tall - 1, 0)

    values = [fields[field] for field in range(FIELDS)]
    for ref, field in ((height, 0), (zonal, 1), (merid, 2)):
        ref[...] = extended(field, values[field])
    statics[0] = extended(3, values[3])
    wet = extended(4, values[4])
    statics[1] = wet * east(wet)
    statics[2] = wet * north(wet)
    deep = extended(5, values[5])
    statics[3] = 0.5 * (deep + east(deep))
    side = pltpu.roll(from_north[(FIELDS + 2) * HALO : (FIELDS + 3) * HALO, :], 128 - PITCH * 5, 1)
    above = jnp.concatenate([from_north[(FIELDS + 1) * HALO : (FIELDS + 2) * HALO, :], side], axis=1)
    last = lax.broadcasted_iota(jnp.int32, (tall, 256), 0) == tall - 1
    upper = jnp.where(last, above[:1], north(deep))
    statics[4] = 0.5 * (deep + upper)
    there = from_north[(FIELDS + 3) * HALO :, :]
    there = jnp.concatenate([there, there], axis=1)
    row = lax.broadcasted_iota(jnp.int32, (8, 256), 0)

    def one_step():
        def shifted_south(value, below):
            return jnp.where(row == 0, pltpu.roll(below, 1, 0), pltpu.roll(value, 1, 0))

        def shifted_north(value, above):
            return jnp.where(row == 7, pltpu.roll(above, 7, 0), pltpu.roll(value, 7, 0))

        before = None
        for first in range(0, tall, 8):
            span = slice(first, first + 8)
            flow, across = zonal[span, :], merid[span, :]
            flux = statics[3, span, :] * flow
            drop = statics[4, span, :] * across
            sums = across + east(across)
            low = before or dict(drop=drop, sums=sums)
            high = height[span, :] - (flux - west(flux)) - (drop - shifted_south(drop, low["drop"]))
            if first == tall - HALO:
                high = high * there
            vbar = 0.25 * (sums + shifted_south(sums, low["sums"]))
            flow = statics[1, span, :] * (flow - (east(high) - high) + statics[0, span, :] * vbar)
            height[span, :] = high
            zonal[span, :] = flow
            now = dict(drop=drop, sums=sums, high=high, pairs=flow + west(flow), across=across, span=span)
            if before:
                finish_merid(before, now["high"], now["pairs"], shifted_north)
            before = now
        finish_merid(before, before["high"], before["pairs"], shifted_north)

    def finish_merid(rows_here, high_above, pairs_above, shifted_north):
        high, pairs_here, span = rows_here["high"], rows_here["pairs"], rows_here["span"]
        ubar = 0.25 * (pairs_here + shifted_north(pairs_here, pairs_above))
        slope = shifted_north(high, high_above) - high
        merid[span, :] = statics[2, span, :] * (rows_here["across"] - slope - statics[0, span, :] * ubar)

    def some_steps(turn, carry):
        for _ in range(STEPS // SNAPS):
            one_step()
        for index, ref in enumerate((height, zonal, merid)):
            place = pl.ds(index * rows * 8 + turn, rows, stride=8)
            frames[place, :] = ref[HALO : HALO + rows, :128]
        return carry

    frames[...] = jnp.zeros(frames.shape, jnp.float32)

    lax.fori_loop(0, SNAPS, some_steps, 0)
    for index, ref in enumerate((height, zonal, merid)):
        state[index] = ref[HALO : HALO + rows, :128]
    snaps[...] = frames[...].reshape(snaps.shape).astype(jnp.bfloat16)

    total = jnp.zeros((8, RANK + 8), jnp.float32)
    for field in range(3):
        for first in range(0, rows, 8):
            frame = rows_of(snaps, field * rows + first)
            tile = jnp.concatenate([rows_of(turned, field * rows + first), frame], axis=0)
            total = total + over_lanes(frame, tile)
    pack_sums(gram[...], total, sums)


def triangle(shape):
    row, lane = (lax.broadcasted_iota(jnp.int32, shape, axis) for axis in (0, 1))
    return lane - shape[0] - row, (lane >= shape[0]) & (lane < 2 * shape[0])


def pack_sums(gram, cross, sums):
    half = RANK // 2
    wide = jnp.concatenate([gram, jnp.zeros((RANK, RANK), jnp.float32)], axis=1)
    apart, there = triangle((half, 128))
    first = pltpu.roll(wide[:half], half, 1)
    block = jnp.where(there, jnp.where(apart >= 0, first, wide[half:]), pltpu.roll(first, RANK, 1))
    block = jnp.where(there | (apart < 0), block, 0.0)
    sums[: half // 2, :] = block[: half // 2] + pltpu.roll(block[half // 2 :], RANK, 1)
    diagonal = jnp.sum(jnp.where(there & (apart == 0), wide[half:], 0.0), axis=0, keepdims=True)
    cross = jnp.concatenate([cross, jnp.zeros((8, 128 - RANK - 8), jnp.float32)], axis=1)
    row = lax.broadcasted_iota(jnp.int32, cross.shape, 0)
    sums[half // 2 :, :] = jnp.where(row < SNAPS, cross, jnp.where(row == SNAPS, diagonal, 0.0))


def unpacked(sums):
    half = RANK // 2
    upper = sums[: half // 2]
    block = jnp.concatenate([upper, pltpu.roll(upper, RANK, 1)], axis=0)
    lane = lax.broadcasted_iota(jnp.int32, block.shape, 1)
    apart, there = triangle(block.shape)
    rest = sums[half // 2 :]
    first = jnp.where(there, jnp.where(apart > 0, block, jnp.where(apart == 0, 0.5 * block, 0.0)), 0.0)
    first = pltpu.roll(first, 128 - half, 1) + jnp.where(there, pltpu.roll(block, half, 1), 0.0)
    diagonal = jnp.where(there & (apart == 0), 0.5 * rest[SNAPS : SNAPS + 1], 0.0)
    second = jnp.where(there & (apart < 0), block, diagonal)
    row = lax.broadcasted_iota(jnp.int32, rest.shape, 0)
    lane = lax.broadcasted_iota(jnp.int32, rest.shape, 1)
    third = jnp.where(row < SNAPS, jnp.where(lane < RANK, rest, 0.5 * rest), 0.0)
    third = jnp.where(lane < KCOLS, third, 0.0)
    beyond = jnp.zeros((128 - RANK - 8, 128), jnp.float32)
    matrix = jnp.concatenate([first, second, third, beyond], axis=0)
    return matrix + jnp.transpose(matrix, (1, 0))


def pairs(offset, around):
    partners = [(i, (((i - offset) ^ 1) + offset) % 16) for i in range(16)]
    return [(i, j) for i, j in partners if around or abs(i - j) == 1]


def window(surface, depth, coriolis, land_sea, basis):
    rows, cols = depth.shape
    whole = pltpu.CompilerParams(vmem_limit_bytes=VMEM_LIMIT)
    fields = jnp.pad(surface, ((0, FIELDS - 3), (0, 0), (0, 0)))
    for field, value in ((3, coriolis), (4, land_sea), (5, depth)):
        around = ((field, FIELDS - 1 - field), (0, 0), (0, 0))
        fields = fields + jnp.pad(value[None], around).astype(jnp.float32)
    packed = pl.pallas_call(
        pack_kernel,
        out_shape=jax.ShapeDtypeStruct((rows, cols), jnp.float32),
        compiler_params=whole,
    )(fields)
    basis, packed = lax.optimization_barrier((basis, packed))
    sides = [lax.ppermute(packed, "gx", pairs(offset, True)) for offset in (0, 1)]

    early = seen_by_kernel(basis, 55 * 1024 * 1024)
    early, sides[0] = lax.optimization_barrier((early, sides[0]))
    basis, early = lax.optimization_barrier((basis, early))
    late = seen_by_kernel(basis)
    basis, late = lax.optimization_barrier((basis, late))
    turned = jnp.transpose(basis, (1, 2, 0, 3)).reshape(3 * rows, RANK, cols)
    turned, sides[1], late = lax.optimization_barrier((turned, sides[1], late))

    def strips(height, index):
        side = pl.BlockSpec((height, cols), lambda i: (index, 0))
        return [pl.BlockSpec((FIELDS, height, cols), lambda i: (0, index, 0)), side, side]

    slab = jax.ShapeDtypeStruct(((FIELDS + 4) * HALO, cols), jnp.float32)
    sends = pl.pallas_call(
        rows_kernel,
        grid=(1,),
        in_specs=strips(2 * HALO, 0) + strips(HALO, rows // HALO - 1),
        out_shape=(slab, slab),
        compiler_params=whole,
    )(fields, *sides, fields, *sides)
    slabs = [lax.ppermute(send, "gy", pairs(offset, False)) for offset, send in enumerate(sends)]
    turned, slabs[0] = lax.optimization_barrier((turned, slabs[0]))
    gram = lax.dot_general(
        turned, turned, (((0, 2), (0, 2)), ((), ())), preferred_element_type=jnp.float32
    )
    gram, slabs = lax.optimization_barrier((gram, slabs))
    tall = (rows + 2 * HALO, 2 * cols)
    final_state, snaps, sums = pl.pallas_call(
        window_kernel,
        out_shape=(
            jax.ShapeDtypeStruct((3, rows, cols), jnp.float32),
            jax.ShapeDtypeStruct((3 * rows, 8, cols), jnp.bfloat16),
            jax.ShapeDtypeStruct((RANK // 4 + 8, 128), jnp.float32),
        ),
        scratch_shapes=[pltpu.VMEM(tall, jnp.float32)] * 3
        + [pltpu.VMEM((5,) + tall, jnp.float32), pltpu.VMEM((3 * rows * 8, cols), jnp.float32)],
        compiler_params=whole,
    )(fields, *sides, *slabs, turned, gram, early, late)
    return final_state, snaps, turned, sums


def exchanged(value, axis, partner):
    return lax.ppermute(value, axis, [(i, partner(i)) for i in range(16)])


def quad_sum(value, axis, one, two):
    first = exchanged(value, axis, lambda i: i ^ one)
    second = exchanged(value, axis, lambda i: i ^ two)
    third = exchanged(value, axis, lambda i: i ^ one ^ two)
    return (value + first) + (second + third)


def total_over_devices(value):
    value = quad_sum(value, "gx", 1, 4)
    value = quad_sum(value, "gx", 3, 12)
    value = quad_sum(value, "gy", 1, 2)
    ring = lambda a: ((a - 1) ^ 1) + 1 if 0 < a < 7 else 7 - a
    value = value + exchanged(value, "gy", lambda i: ring(i // 2) * 2 + i % 2)
    ring = lambda a: (7 - a) if a in (1, 2, 5, 6) else {0: 3, 3: 0, 4: 7, 7: 4}[a]
    return value + exchanged(value, "gy", lambda i: ring(i // 2) * 2 + i % 2)


ORDERS = ((0, 0), (0, 1), (1, 0), (0, 2), (1, 1), (2, 0))
PITCH_OF_SWEEP = 176
LEAD = 56
GROUPS = ((0, 32), (32, 32))


def parts_of(value):
    parts = []
    for _ in range(3):
        parts.append(value.astype(jnp.bfloat16))
        value = value - parts[-1].astype(jnp.float32)
    return parts


def parts_dot(left, right, count, turned=False):
    left = jnp.concatenate([left[i] for i, _ in ORDERS[:count]], axis=1)
    right = jnp.concatenate([right[j] for _, j in ORDERS[:count]], axis=1 if turned else 0)
    return lax.dot_general(
        left, right, (((1,), (1 if turned else 0,)), ((), ())), preferred_element_type=jnp.float32
    )


def refine(gram, start, store):
    blocks = RANK // 8
    sweep = lax.broadcasted_iota(jnp.int32, (8, 128), 0)
    gram = parts_of(gram)
    made = None
    for time in range(blocks + SUBITER - 1):
        inputs = []
        for i in range(8):
            value = jnp.zeros((8, 128), jnp.float32) if made is None else pltpu.roll(made[i], 1, 0)
            if time < blocks:
                value = jnp.where(sweep == 0, start[8 * time + i : 8 * time + i + 1, :], value)
            inputs.append(value)
        active = (sweep <= time) & (sweep > time - blocks) & (sweep < SUBITER)
        images = parts_dot(parts_of(jnp.concatenate(inputs, axis=0)), gram, 6)
        running = [k for k in range(SUBITER) if 0 < time - k < blocks]
        if running:
            history = [store[pl.ds(k * PITCH_OF_SWEEP + LEAD, 8 * (time - k)), :] for k in running]
            length = sum(rows.shape[0] for rows in history)
            if length % 128:
                history.append(jnp.zeros((128 - length % 128, 128), jnp.float32))
            history = parts_of(jnp.concatenate(history, axis=0))
            inner = parts_dot(parts_of(images), history, 3, turned=True)
            row = lax.broadcasted_iota(jnp.int32, inner.shape, 0) & 7
            col = lax.broadcasted_iota(jnp.int32, inner.shape, 1)
            owner, edge = jnp.full(inner.shape, running[0], jnp.int32), 0
            for k in running[:-1]:
                edge += 8 * (time - k)
                owner = owner + jnp.where(col >= edge, 1, 0)
            inner = jnp.where(row == owner, inner, 0.0)
            images = images - parts_dot(parts_of(inner), history, 5)
        parts = [images[8 * i : 8 * i + 8] for i in range(8)]
        square = {
            (i, j): jnp.sum(parts[i] * parts[j], axis=1, keepdims=True)
            for i in range(8)
            for j in range(i, 8)
        }
        made = []
        for i in range(8):
            scale = lax.rsqrt(square[i, i])
            unit = parts[i] * scale
            made.append(jnp.where(active, unit, 0.0))
            lower = {j: square[i, j] * scale for j in range(i + 1, 8)}
            for j in range(i + 1, 8):
                parts[j] = parts[j] - lower[j] * unit
                for p in range(j, 8):
                    square[j, p] = square[j, p] - lower[j] * lower[p]
        for i in range(8):
            store[pl.ds(LEAD + 8 * time + i, 8, stride=PITCH_OF_SWEEP - 8), :] = made[i]
        yield time


def finish_kernel(
    sums, outer, start, weights, snaps, turned, projected, out, store, store_sems
):
    rows = out.shape[2]
    stores = [
        [
            pltpu.make_async_copy(
                out.at[pl.ds(first, size), f], projected.at[pl.ds(first, size), f], store_sems.at[3 * index + f]
            )
            for f in range(3)
        ]
        for index, (first, size) in enumerate(GROUPS)
    ]
    bands = [(f, first, min(16, rows - first)) for f in range(3) for first in range(0, rows, 16)]
    gram = unpacked(sums[...])

    def mix_of(index):
        first, size = GROUPS[index]
        rows_of_mix = store[pl.ds((SUBITER - 1) * PITCH_OF_SWEEP + LEAD + first, size), :] * weights[...]
        return rows_of_mix[:, : RANK + 8].astype(jnp.bfloat16)

    def mixed(index, mix, field, first, count):
        made, size = GROUPS[index]
        done = []
        for h in range(count // 8):
            spot = field * rows + first + 8 * h
            tile = jnp.concatenate([rows_of(turned, spot), rows_of(snaps, spot)], axis=0)
            total = jnp.dot(mix, tile, preferred_element_type=jnp.float32)
            parts = [total[:, 128 * i : 128 * i + 128].reshape(size // 8, 8, 128) for i in range(8)]
            done.append(jnp.stack(crossed(parts), axis=1).reshape(size, 8, 128))
        done = done[0] if count == 8 else jnp.concatenate(done, axis=1)
        out[made : made + size, field, first : first + count, :] = done.astype(jnp.bfloat16)
        if first + count == rows:
            stores[index][field].start()

    last = RANK // 8 + SUBITER - 2
    ready = [SUBITER - 2 + (first + size) // 8 for first, size in GROUPS]
    work = []
    for time in refine(gram * outer[...], start, store):
        for index, due in enumerate(ready):
            if time == due:
                mix = mix_of(index)
                work += [(index, mix, *band) for band in bands]
        if time < last:
            until = min([due for due in ready if due > time])
            now = -(-len(work) // (until - time))
            for item in work[:now]:
                mixed(*item)
            work = work[now:]
    for item in work:
        mixed(*item)
    for group in stores:
        for copy in group:
            copy.wait()


def local(surface, depth, coriolis, land_sea, basis, energies, start):
    rows, cols = depth.shape
    final_state, snaps, turned, sums = window(surface, depth, coriolis, land_sea, basis)
    sums = total_over_devices(sums)
    cells = 3.0 * rows * cols * lax.axis_size("gx") * lax.axis_size("gy")
    weights = jnp.concatenate([energies, jnp.ones((SNAPS,), jnp.float32)])
    weights = jnp.pad(weights, (0, 128 - KCOLS))
    outer = weights[:, None] * weights[None, :] / cells
    begin = jnp.pad(start.T, ((0, 0), (0, 128 - KCOLS)))
    vmem = pl.BlockSpec(memory_space=pltpu.VMEM)
    projected = pl.pallas_call(
        finish_kernel,
        in_specs=[vmem] * 6,
        out_specs=pl.BlockSpec(memory_space=pl.ANY),
        out_shape=jax.ShapeDtypeStruct(basis.shape, jnp.bfloat16),
        scratch_shapes=[
            pltpu.VMEM(basis.shape, jnp.bfloat16),
            pltpu.VMEM((8 * PITCH_OF_SWEEP, 128), jnp.float32),
            pltpu.SemaphoreType.DMA((3 * len(GROUPS),)),
        ],
        compiler_params=pltpu.CompilerParams(vmem_limit_bytes=VMEM_LIMIT),
    )(sums, outer, begin, weights[None, :], snaps, turned)
    return (final_state, projected)


def solution(mesh):
    placed = (
        P(None, "gy", "gx"),
        P("gy", "gx"),
        P("gy", "gx"),
        P("gy", "gx"),
        P(None, None, "gy", "gx"),
        P(),
        P(),
    )
    return jax.shard_map(
        local,
        mesh=mesh,
        in_specs=placed,
        out_specs=(P(None, "gy", "gx"), P(None, None, "gy", "gx")),
        check_vma=False,
    )
```
